256 devices in a mesh: dp: 32 (over z, y), mp: 8 (over x, core).
Axes of the slice: x: 4, y: 4, z: 8, core: 2. Of those that a mesh axis runs over, the one named last changes fastest.
Arguments:
- tokens: bfloat16 [12288, 4096], P(('dp', 'mp')), may hold values from -8 to 8
- encoded: bfloat16 [128, 128, 1024], P('dp'), may hold values from -8 to 8
- neighbour_owner: int32 [32, 6, 2], replicated, may hold values from 0 to 31, as said below
- neighbour_slot: int32 [32, 6, 2], replicated, may hold values from 0 to 3
- w_query: bfloat16 [4096, 4096], P(None, 'mp'), may hold values from -0.09375 to 0.09375
- w_key: bfloat16 [1024, 4096], P(None, 'mp'), may hold values from -0.1875 to 0.1875
- w_value: bfloat16 [1024, 4096], P(None, 'mp'), may hold values from -0.1875 to 0.1875
- w_out: bfloat16 [4096, 4096], P('mp'), may hold values from -0.09375 to 0.09375
- grad_out: bfloat16 [12288, 4096], P(('dp', 'mp')), may hold values from -6 to 6
Outputs:
- attended: bfloat16 [12288, 4096], P(('dp', 'mp'))
- grad_tokens: bfloat16 [12288, 4096], P(('dp', 'mp'))
- grad_encoded: float32 [128, 128, 1024], P('dp', None, 'mp')
The draws below stay inside these ranges and needn't reach their ends.
Inputs may be any that keep to these rules, and one draw needn't show every extreme that they name: `neighbour_owner`: within one sequence's list no owner appears twice, and the list of sequence s names owner s.
All inputs are finite; a program needn't handle non-finite values.
Results may differ from the reference program's by a relative error of at most 0.017.
Values may be sent and summed in bfloat16 or wider, within the bound.
No kernel may reach another device: no remote copies, remote signals or barrier semaphores. Data moves between devices by JAX's collectives and lax.ppermute only.
A program may use at most 128 MiB of HBM per device.

```python
import math
import jax
import jax.numpy as jnp
from jax import lax

D = 4096
HEADS = 32
HD = 128
DE = 1024
GROUP = 64
NBR = 2
NLEN = 128
POOL_DEV = 4
GROUPS = 6
LEN = 384
NEIGH = 12
SEQS = 32
POOL = 128


def rough_rows(key, shape):
    first = jax.random.fold_in(key, 0)
    base = jax.random.normal(first, shape, jnp.float32)
    base = jnp.clip(base, -6.0, 6.0)
    return base


def draw_tokens(key, part):
    key = jax.random.fold_in(key, 21)
    return rough_rows(key, (SEQS * LEN, D)).astype(jnp.bfloat16)


def draw_encoded(key, part):
    key = jax.random.fold_in(key, 22)
    return rough_rows(key, (POOL, NLEN, DE)).astype(jnp.bfloat16)


def draw_neighbour_owner(key, part):
    key = jax.random.fold_in(key, 11)
    first, second = jax.random.split(key)
    favour = jax.random.randint(first, (SEQS,), 0, 4)
    noise = jax.random.randint(second, (SEQS, SEQS), 0, 1024)
    scores = noise + 600 * favour[None, :]
    own = jnp.arange(SEQS)[:, None] == jnp.arange(SEQS)[None, :]
    scores = jnp.where(own, 1 << 20, scores)
    scores = scores * SEQS + jnp.arange(SEQS)[None, :]
    chosen = lax.top_k(scores, NEIGH)[1]
    return chosen.astype(jnp.int32).reshape(SEQS, GROUPS, NBR)


def draw_neighbour_slot(key, part):
    key = jax.random.fold_in(key, 12)
    slots = jax.random.randint(key, (SEQS, NEIGH), 0, POOL_DEV)
    slots = slots.at[0, 0].set(POOL_DEV - 1).at[0, 1].set(0)
    return slots.astype(jnp.int32).reshape(SEQS, GROUPS, NBR)


def levels(stream_key, extent, pieces, low, top_value):
    def one(axis_at, parts):
        draws = jax.random.uniform(jax.random.fold_in(jax.random.fold_in(stream_key, 6), axis_at), (parts,), jnp.float32, low / len(pieces), top_value / len(pieces))
        return jnp.repeat(jnp.exp(draws), extent[axis_at] // parts).reshape((-1,) + (1,) * (len(extent) - axis_at - 1))

    gain = one(*pieces[0])
    for cut in pieces[1:]:
        gain = gain * one(*cut)
    return gain


def normal_values(key, shape, deviation, limit, pieces=(), dtype=jnp.bfloat16):
    gain = levels(key, shape, pieces, -0.22, 0.18) if pieces else 1.0
    array = jax.random.normal(key, shape, jnp.float32) * deviation * gain
    return jnp.minimum(jnp.maximum(array, -limit), limit).astype(dtype)


def setup_inputs(seed: int = 0) -> dict:
    splits = jax.random.split(jax.random.key(seed), 10)
    tokens = draw_tokens(jax.random.fold_in(splits[9], 71), 0)
    encoded = draw_encoded(jax.random.fold_in(splits[9], 71), 0)
    neighbour_owner = draw_neighbour_owner(jax.random.fold_in(splits[9], 71), 0)
    neighbour_slot = draw_neighbour_slot(jax.random.fold_in(splits[9], 71), 0)
    w_query = normal_values(splits[4], (D, D), D ** -0.5, 0.09375, ((1, 8),))
    w_key = normal_values(splits[5], (DE, D), DE ** -0.5, 0.1875, ((1, 8),))
    w_value = normal_values(splits[6], (DE, D), DE ** -0.5, 0.1875, ((1, 8),))
    w_out = normal_values(splits[7], (D, D), D ** -0.5, 0.09375, ((0, 8),))
    grad_out = normal_values(splits[8], (SEQS * LEN, D), 1.0, 6.0, ((0, 256),))
    return {"tokens": tokens, "encoded": encoded, "neighbour_owner": neighbour_owner, "neighbour_slot": neighbour_slot, "w_query": w_query, "w_key": w_key, "w_value": w_value, "w_out": w_out, "grad_out": grad_out}


def reference(tokens, encoded, neighbour_owner, neighbour_slot, w_query, w_key, w_value, w_out, grad_out):
    score_scale = 1.0 / math.sqrt(HD)

    def one_sequence(totals, items):
        rows_in, grad_in, owners, slots = items
        taken = (owners * POOL_DEV + slots).reshape(-1).astype(jnp.int32)
        nearby = encoded[taken].reshape(NEIGH * NLEN, DE)
        query = jnp.dot(rows_in, w_query, preferred_element_type=jnp.float32).astype(jnp.bfloat16)
        key_rows = jnp.dot(nearby, w_key, preferred_element_type=jnp.float32).astype(jnp.bfloat16)
        value_rows = jnp.dot(nearby, w_value, preferred_element_type=jnp.float32).astype(jnp.bfloat16)
        query_blocks = query.reshape(GROUPS, GROUP, HEADS, HD).astype(jnp.float32)
        key_blocks = key_rows.reshape(GROUPS, NBR * NLEN, HEADS, HD).astype(jnp.float32)
        value_blocks = value_rows.reshape(GROUPS, NBR * NLEN, HEADS, HD).astype(jnp.float32)
        scores = jnp.einsum('cqhe,ckhe->chqk', query_blocks, key_blocks) * score_scale
        probs = jax.nn.softmax(scores, axis=-1)
        probs_b = probs.astype(jnp.bfloat16).astype(jnp.float32)
        heads_out = jnp.einsum('chqk,ckhe->cqhe', probs_b, value_blocks).astype(jnp.bfloat16).reshape(LEN, D)
        attended = jnp.dot(heads_out, w_out, preferred_element_type=jnp.float32).astype(jnp.bfloat16)
        grad_heads = jnp.dot(grad_in, w_out.T, preferred_element_type=jnp.float32).astype(jnp.bfloat16)
        grad_blocks = grad_heads.reshape(GROUPS, GROUP, HEADS, HD).astype(jnp.float32)
        grad_probs = jnp.einsum('cqhe,ckhe->chqk', grad_blocks, value_blocks)
        centre = lax.optimization_barrier(jnp.sum(probs * grad_probs, axis=-1, keepdims=True))
        grad_scores = (probs * (grad_probs - centre) * score_scale).astype(jnp.bfloat16).astype(jnp.float32)
        grad_query = jnp.einsum('chqk,ckhe->cqhe', grad_scores, key_blocks).astype(jnp.bfloat16).reshape(LEN, D)
        grad_keys = jnp.einsum('chqk,cqhe->ckhe', grad_scores, query_blocks).astype(jnp.bfloat16).reshape(NEIGH * NLEN, D)
        grad_values = jnp.einsum('chqk,cqhe->ckhe', probs_b, grad_blocks).astype(jnp.bfloat16).reshape(NEIGH * NLEN, D)
        grad_rows = jnp.dot(grad_query, w_query.T, preferred_element_type=jnp.float32).astype(jnp.bfloat16)
        grad_nearby = jnp.dot(grad_keys, w_key.T, preferred_element_type=jnp.float32) + jnp.dot(grad_values, w_value.T, preferred_element_type=jnp.float32)
        totals = totals.at[taken].add(grad_nearby.reshape(NEIGH, NLEN, DE))
        return (totals, (attended, grad_rows))
    start_total = jnp.zeros((POOL, NLEN, DE), jnp.float32)
    items = (tokens.reshape(SEQS, LEN, D), grad_out.reshape(SEQS, LEN, D), neighbour_owner, neighbour_slot)
    grad_encoded, (attended, grad_tokens) = lax.scan(one_sequence, start_total, items)
    return (attended.reshape(SEQS * LEN, D), grad_tokens.reshape(SEQS * LEN, D), grad_encoded)
```

```python
import functools
import math

import jax
import jax.numpy as jnp
from jax import lax
from jax.experimental import pallas as pl
from jax.experimental.pallas import tpu as pltpu
from jax.sharding import PartitionSpec as P

HD = 128
GROUP = 64
NBR = 2
XS = 4
CORES = 2
BF = jnp.bfloat16
F32 = jnp.float32
NT = (((1,), (1,)), ((), ()))
TN = (((0,), (0,)), ((), ()))


def mm(a, b):
    return jnp.dot(a, b, preferred_element_type=F32)


def mm_nt(a, b):
    return lax.dot_general(a, b, NT, preferred_element_type=F32)


def mm_tn(a, b):
    return lax.dot_general(a, b, TN, preferred_element_type=F32)


def x_perm(step):
    return [(2 * x + c, 2 * ((x + step) % XS) + c) for x in range(XS) for c in range(CORES)]


CORE_SWAP = [(2 * x + c, 2 * x + 1 - c) for x in range(XS) for c in range(CORES)]


def gather_pieces(block):
    own = [block]
    for step in (1, -1, 2):
        own.append(lax.ppermute(block, "mp", x_perm(step)))
    other = [lax.ppermute(piece, "mp", CORE_SWAP) for piece in own]
    return own + other


def piece_owners(x, c):
    own = [2 * ((x + XS - step) % XS) + c for step in (0, 1, -1, 2)]
    other = [2 * ((x + XS - step) % XS) + 1 - c for step in (0, 1, -1, 2)]
    return jnp.stack(own + other).astype(jnp.int32)


def project_kernel(owner_ref, *refs):
    t_refs, g_refs = refs[:8], refs[8:16]
    wq_ref, wo_ref, q_ref, gh_ref, q_acc, gh_acc = refs[16:]
    step = pl.program_id(0)
    t = jnp.concatenate([r[...] for r in t_refs], axis=0)
    g = jnp.concatenate([r[...] for r in g_refs], axis=0)
    dq = mm(t, wq_ref[...])
    dg = mm_nt(g, wo_ref[...])

    @pl.when(step == 0)
    def _():
        q_acc[...] = dq
        gh_acc[...] = dg

    @pl.when(step > 0)
    def _():
        q_acc[...] += dq
        gh_acc[...] += dg

    @pl.when(step == pl.num_programs(0) - 1)
    def _():
        rows = t_refs[0].shape[0]
        for j in range(8):
            at = pl.ds(pl.multiple_of(owner_ref[j] * rows, rows), rows)
            q_ref[at, :] = q_acc[j * rows : (j + 1) * rows, :].astype(BF)
            gh_ref[at, :] = gh_acc[j * rows : (j + 1) * rows, :].astype(BF)


def project(owners, t_pieces, g_pieces, w_query, w_out):
    rows, depth = t_pieces[0].shape
    width = w_query.shape[1]
    cut = 512
    piece = pl.BlockSpec((rows, cut), lambda i, s: (0, i))
    whole = pl.BlockSpec((8 * rows, width), lambda i, s: (0, 0))
    out = jax.ShapeDtypeStruct((8 * rows, width), BF)
    return pl.pallas_call(
        project_kernel,
        grid_spec=pltpu.PrefetchScalarGridSpec(
            num_scalar_prefetch=1,
            grid=(depth // cut,),
            in_specs=[piece] * 16
            + [
                pl.BlockSpec((cut, width), lambda i, s: (i, 0)),
                pl.BlockSpec((width, cut), lambda i, s: (0, i)),
            ],
            out_specs=[whole, whole],
            scratch_shapes=[pltpu.VMEM((8 * rows, width), F32)] * 2,
        ),
        out_shape=[out, out],
        compiler_params=pltpu.CompilerParams(vmem_limit_bytes=24 << 20),
        cost_estimate=pl.CostEstimate(
            flops=4 * 8 * rows * depth * width, bytes_accessed=15 << 20, transcendentals=0
        ),
        name="project",
    )(owners, *t_pieces, *g_pieces, w_query, w_out)


def attend_kernel(owner_ref, *refs):
    p_refs = refs[:8]
    q_ref, gh_ref, wk_ref, wv_ref, ho_ref, gq_ref, keep_ref, send_ref, near, grad = refs[8:]
    heads = q_ref.shape[1] // HD
    scale = 1.0 / math.sqrt(HD)
    keys = near.shape[0]
    for j in range(8):
        at = pl.ds(pl.multiple_of(owner_ref[j] * 128, 128), 128)
        near[:, at] = p_refs[j][...].reshape(keys, 128)
    rows = near[...]
    k = mm(rows, wk_ref[...]).astype(BF)
    v = mm(rows, wv_ref[...]).astype(BF)
    q = q_ref[...]
    gh = gh_ref[...]
    part = [slice(h * HD, (h + 1) * HD) for h in range(heads)]
    s = jnp.concatenate([mm_nt(q[:, p], k[:, p]) for p in part], axis=0) * scale
    gp = jnp.concatenate([mm_nt(gh[:, p], v[:, p]) for p in part], axis=0)
    e = jnp.exp(s - jnp.max(s, axis=-1, keepdims=True))
    probs = e * (1.0 / jnp.sum(e, axis=-1, keepdims=True))
    pb = probs.astype(BF)
    centre = jnp.sum(probs * gp, axis=-1, keepdims=True)
    gs = (probs * (gp - centre) * scale).astype(BF)
    gk = []
    gv = []
    for h, p in enumerate(part):
        r = slice(h * GROUP, (h + 1) * GROUP)
        ho_ref[:, p] = mm(pb[r], v[:, p]).astype(BF)
        gq_ref[:, p] = mm(gs[r], k[:, p]).astype(BF)
        gk.append(mm_tn(gs[r], q[:, p]).astype(BF))
        gv.append(mm_tn(pb[r], gh[:, p]).astype(BF))
    gk = jnp.concatenate(gk, axis=1)
    gv = jnp.concatenate(gv, axis=1)
    grad[...] = mm_nt(gk, wk_ref[...]) + mm_nt(gv, wv_ref[...])
    for step in range(XS):
        mine = pl.ds(pl.multiple_of(owner_ref[8 + step] * 128, 128), 128)
        keep_ref[step] = grad[:, mine].astype(BF).reshape(keep_ref.shape[1:])
        sibling = pl.ds(pl.multiple_of(owner_ref[8 + XS + step] * 128, 128), 128)
        send_ref[step] = grad[:, sibling].astype(BF).reshape(send_ref.shape[1:])


def attend(indices, pieces, q, gh, w_key, w_value):
    neigh, depth, cols = pieces[0].shape
    length, width = q.shape
    groups = length // GROUP
    piece = pl.BlockSpec((NBR, depth, cols), lambda i, s: (i, 0, 0))
    rows = pl.BlockSpec((GROUP, width), lambda i, s: (i, 0))
    weight = pl.BlockSpec(w_key.shape, lambda i, s: (0, 0), pipeline_mode=pl.Buffered(1))
    share = pl.BlockSpec((XS, NBR, depth, cols), lambda i, s: (0, i, 0, 0))
    small = jax.ShapeDtypeStruct((length, width), BF)
    half = jax.ShapeDtypeStruct((XS, neigh, depth, cols), BF)
    return pl.pallas_call(
        attend_kernel,
        grid_spec=pltpu.PrefetchScalarGridSpec(
            num_scalar_prefetch=1,
            grid=(groups,),
            in_specs=[piece] * 8 + [rows, rows, weight, weight],
            out_specs=[rows, rows, share, share],
            scratch_shapes=[
                pltpu.VMEM((NBR * depth, 8 * cols), BF),
                pltpu.VMEM((NBR * depth, 8 * cols), F32),
            ],
        ),
        out_shape=[small, small, half, half],
        compiler_params=pltpu.CompilerParams(vmem_limit_bytes=32 << 20),
        cost_estimate=pl.CostEstimate(
            flops=8 * neigh * depth * 8 * cols * width,
            bytes_accessed=12 << 20,
            transcendentals=length * 4 * NBR * depth,
        ),
        name="attend",
    )(indices, *pieces, q, gh, w_key, w_value)


def out_kernel(index_ref, a_ref, w_ref, keep_ref, send_ref, *, transposed):
    rows = keep_ref.shape[1]
    blocks = []
    for j in range(8):
        at = pl.ds(pl.multiple_of(index_ref[8 + j] * rows, rows), rows)
        blocks.append(a_ref[at, :])
    a = jnp.concatenate(blocks, axis=0)
    r = (mm_nt if transposed else mm)(a, w_ref[...]).astype(BF)
    keep_ref[...] = r[: XS * rows].reshape(keep_ref.shape)
    send_ref[...] = r[XS * rows :].reshape(send_ref.shape)


def out_project(indices, a, w, transposed, name):
    length, width = a.shape
    full = w.shape[0] if transposed else w.shape[1]
    rows = length // 8
    cut = 1024
    if transposed:
        weight = pl.BlockSpec((cut, width), lambda i, s: (i, 0))
    else:
        weight = pl.BlockSpec((width, cut), lambda i, s: (0, i))
    half_spec = pl.BlockSpec((XS, rows, cut), lambda i, s: (0, 0, i))
    half = jax.ShapeDtypeStruct((XS, rows, full), BF)
    return pl.pallas_call(
        functools.partial(out_kernel, transposed=transposed),
        grid_spec=pltpu.PrefetchScalarGridSpec(
            num_scalar_prefetch=1,
            grid=(full // cut,),
            in_specs=[pl.BlockSpec((length, width), lambda i, s: (0, 0)), weight],
            out_specs=[half_spec, half_spec],
        ),
        out_shape=[half, half],
        compiler_params=pltpu.CompilerParams(vmem_limit_bytes=24 << 20),
        cost_estimate=pl.CostEstimate(
            flops=2 * length * width * full, bytes_accessed=8 << 20, transcendentals=0
        ),
        name=name,
    )(indices, a, w)


def chip_sums(keep, send):
    got = lax.ppermute(send, "mp", CORE_SWAP)
    return [(keep[i].astype(F32) + got[i].astype(F32)).astype(BF) for i in range(XS)]


def x_sum(sums):
    total = sums[0].astype(F32)
    for step in range(1, XS):
        total = total + lax.ppermute(sums[step], "mp", x_perm(step)).astype(F32)
    return total.astype(BF)


def body(
    tokens, encoded, neighbour_owner, neighbour_slot, w_query, w_key, w_value, w_out, grad_out
):
    dp_count = lax.axis_size("dp")
    dp_at = lax.axis_index("dp")
    mp_at = lax.axis_index("mp")
    x, c = mp_at // CORES, mp_at % CORES
    neigh = neighbour_owner.shape[1] * NBR
    share = encoded.shape[2] // (XS * CORES)
    owners = piece_owners(x, c)
    targets = jnp.stack(
        [2 * ((x + i) % XS) + c for i in range(XS)]
        + [2 * ((x + i) % XS) + 1 - c for i in range(XS)]
    ).astype(jnp.int32)
    indices = jnp.concatenate([owners, targets])

    owners_all = neighbour_owner.reshape(dp_count, neigh)
    slots_all = neighbour_slot.reshape(dp_count, neigh)
    held_here = owners_all == dp_at
    wanted = jnp.any(held_here, axis=1)
    held_slot = jnp.sum(jnp.where(held_here, slots_all, 0), axis=1)
    my_owners = lax.dynamic_index_in_dim(owners_all, dp_at, 0, keepdims=False)
    place = jnp.argmax(my_owners[None, :] == jnp.arange(dp_count)[:, None], axis=1)

    t_pieces = gather_pieces(tokens)
    g_pieces = gather_pieces(grad_out)

    mine = lax.dynamic_slice_in_dim(encoded, mp_at * share, share, axis=2)
    arrived = lax.all_to_all(mine[held_slot], "dp", split_axis=0, concat_axis=0, tiled=True)
    n_pieces = gather_pieces(arrived[my_owners])

    query, grad_heads = project(owners, t_pieces, g_pieces, w_query, w_out)
    heads_out, grad_query, n_keep, n_send = attend(
        indices, n_pieces, query, grad_heads, w_key, w_value
    )
    grad_share = x_sum(chip_sums(n_keep, n_send))
    returned = lax.all_to_all(grad_share[place], "dp", split_axis=0, concat_axis=0, tiled=True)

    attended = x_sum(chip_sums(*out_project(indices, heads_out, w_out, False, "attended")))
    grad_tokens = x_sum(chip_sums(*out_project(indices, grad_query, w_query, True, "gtokens")))

    pick = (held_slot[None, :] == jnp.arange(encoded.shape[0])[:, None]) & wanted[None, :]
    grad_encoded = jnp.dot(
        pick.astype(BF), returned.reshape(dp_count, -1), preferred_element_type=F32
    ).reshape(encoded.shape[0], encoded.shape[1], share)
    return (attended, grad_tokens, grad_encoded)


def solution(mesh):
    placed = (
        P(("dp", "mp"), None),
        P("dp", None, None),
        P(),
        P(),
        P(None, "mp"),
        P(None, "mp"),
        P(None, "mp"),
        P("mp", None),
        P(("dp", "mp"), None),
    )
    return jax.shard_map(
        body,
        mesh=mesh,
        in_specs=placed,
        out_specs=(P(("dp", "mp"), None), P(("dp", "mp"), None), P("dp", None, "mp")),
        check_vma=False,
    )
```

```python
import functools
import math

import jax
import jax.numpy as jnp
from jax import lax
from jax.experimental import pallas as pl
from jax.experimental.pallas import tpu as pltpu
from jax.sharding import PartitionSpec as P

HD = 128
GROUP = 64
NBR = 2
XS = 4
CORES = 2
BF = jnp.bfloat16
F32 = jnp.float32
BIG = 56
CHUNKS = 1
FIRST = 16
OUTS = 0.3
LAST = 65536
NT = (((1,), (1,)), ((), ()))
TN = (((0,), (0,)), ((), ()))


def mm(a, b):
    return jnp.dot(a, b, preferred_element_type=F32)


def mm_nt(a, b):
    return lax.dot_general(a, b, NT, preferred_element_type=F32)


def mm_tn(a, b):
    return lax.dot_general(a, b, TN, preferred_element_type=F32)


def x_perm(step):
    return [(2 * x + c, 2 * ((x + step) % XS) + c) for x in range(XS) for c in range(CORES)]


CORE_SWAP = [(2 * x + c, 2 * x + 1 - c) for x in range(XS) for c in range(CORES)]


def x_pieces(block):
    return [block] + [lax.ppermute(block, "mp", x_perm(step)) for step in (1, -1, 2)]


def swap(block):
    return lax.ppermute(block, "mp", CORE_SWAP)


def after(values, earlier):
    return lax.optimization_barrier((values, earlier))[0]


def piece_owners(x, c):
    own = [2 * ((x + XS - step) % XS) + c for step in (0, 1, -1, 2)]
    other = [2 * ((x + XS - step) % XS) + 1 - c for step in (0, 1, -1, 2)]
    return jnp.stack(own + other).astype(jnp.int32)


ANY = pl.BlockSpec(memory_space=pl.ANY)
SMEM = pl.BlockSpec(memory_space=pltpu.SMEM)
VMEM = pl.BlockSpec(memory_space=pltpu.VMEM)


def params(mib):
    return pltpu.CompilerParams(vmem_limit_bytes=mib << 20)


def cost(flops, bytes_accessed):
    return pl.CostEstimate(flops=flops, bytes_accessed=bytes_accessed, transcendentals=0)


def project_kernel(*refs, cut, transposed):
    pieces = refs[:4]
    w_any, wx_any, out_ref, outx_ref, a_ref, w_ref, wx_ref, acc, accx, sems = refs[4:]
    rows = pieces[0].shape[0]
    steps = a_ref.shape[1] // cut
    copies = []
    for j, piece in enumerate(pieces):
        at = pl.ds(j * rows, rows)
        copies.append(pltpu.make_async_copy(piece, a_ref.at[at, :], sems.at[j]))
        copies[-1].start()
    weights = []
    for k in range(steps):
        part = pl.ds(k * cut, cut)
        at = (slice(None), part) if transposed else (part, slice(None))
        weights.append(
            [
                pltpu.make_async_copy(w_any.at[at], w_ref.at[at], sems.at[4 + 2 * k]),
                pltpu.make_async_copy(wx_any.at[at], wx_ref.at[at], sems.at[5 + 2 * k]),
            ]
        )
        for copy in weights[-1]:
            copy.start()
    for copy in copies:
        copy.wait()
    for k in range(steps):
        part = slice(k * cut, (k + 1) * cut)
        a = a_ref[:, part]
        for copy, w, total, out in zip(
            weights[k], (w_ref, wx_ref), (acc, accx), (out_ref, outx_ref)
        ):
            copy.wait()
            add = mm_nt(a, w[:, part]) if transposed else mm(a, w[part, :])
            if k == 0:
                total[...] = add
            elif k < steps - 1:
                total[...] += add
            else:
                out[...] = (total[...] + add).astype(BF)


def project(pieces, w, wx, transposed, name, weight=1):
    rows, depth = pieces[0].shape
    width = w.shape[0] if transposed else w.shape[1]
    length = rows * len(pieces)
    cut = depth // 8
    out = jax.ShapeDtypeStruct((length, width), BF)
    return pl.pallas_call(
        functools.partial(project_kernel, cut=cut, transposed=transposed),
        in_specs=[ANY] * 6,
        out_specs=[VMEM] * 2,
        scratch_shapes=[
            pltpu.VMEM((length, depth), BF),
            pltpu.VMEM(w.shape, BF),
            pltpu.VMEM(w.shape, BF),
            pltpu.VMEM((length, width), F32),
            pltpu.VMEM((length, width), F32),
            pltpu.SemaphoreType.DMA((4 + 2 * (depth // cut),)),
        ],
        out_shape=[out, out],
        compiler_params=params(BIG),
        cost_estimate=cost(int(4 * length * depth * width * weight), 10 << 20),
        name=name,
    )(*pieces, w, wx)


def attend_kernel(index_ref, *refs, first):
    pieces = refs[:8]
    q_own, q_other, gh_own, gh_other, wk_any, wv_any = refs[8:14]
    ho_ref, gq_ref, keep_ref, send_ref, near, q_ref, gh_ref, wk_ref, wv_ref, grad, sems = refs[14:]
    neigh, depth, cols = pieces[0].shape
    groups = neigh // NBR
    keys = NBR * depth
    heads = q_ref.shape[1] // HD
    scale = 1.0 / math.sqrt(HD)
    batch = NBR * math.gcd(groups, 2)
    moves = [(wk_any, wk_ref), (wv_any, wv_ref)]
    rows = q_ref.shape[0] // 8
    for j in range(8):
        at = pl.ds(pl.multiple_of(index_ref[j] * rows, 16), rows)
        part = pl.ds(j % XS * rows, rows)
        moves.append(((q_own, q_other)[j // XS].at[part, :], q_ref.at[at, :]))
        moves.append(((gh_own, gh_other)[j // XS].at[part, :], gh_ref.at[at, :]))
    for n in range(0, neigh, batch):
        for j in range(8):
            at = pl.ds(pl.multiple_of(index_ref[j] * cols, cols), cols)
            part = pl.ds(n, batch)
            moves.append((pieces[j].at[part], near.at[part, :, at]))
    copies = [pltpu.make_async_copy(s, d, sems.at[i]) for i, (s, d) in enumerate(moves)]
    for copy in copies:
        copy.start()
    for copy in copies[:18]:
        copy.wait()
    part = [slice(h * HD, (h + 1) * HD) for h in range(heads)]
    for g in range(groups):
        own = slice(g * GROUP, (g + 1) * GROUP)
        there = slice((first + g) * GROUP, (first + g + 1) * GROUP)
        two = slice(g * NBR, (g + 1) * NBR)
        if g * NBR % batch == 0:
            for copy in copies[18 + g * NBR // batch * 8 :][:8]:
                copy.wait()
        rows = near[two].reshape(keys, near.shape[2])
        k = mm(rows, wk_ref[...]).astype(BF)
        v = mm(rows, wv_ref[...]).astype(BF)
        q = q_ref[there, :]
        gh = gh_ref[there, :]
        s = jnp.concatenate([mm_nt(q[:, p], k[:, p]) for p in part], axis=0) * scale
        gp = jnp.concatenate([mm_nt(gh[:, p], v[:, p]) for p in part], axis=0)
        e = jnp.exp(s - jnp.max(s, axis=-1, keepdims=True))
        probs = e * (1.0 / jnp.sum(e, axis=-1, keepdims=True))
        pb = probs.astype(BF)
        centre = jnp.sum(probs * gp, axis=-1, keepdims=True)
        gs = (probs * (gp - centre) * scale).astype(BF)
        gk = []
        gv = []
        for h, p in enumerate(part):
            r = slice(h * GROUP, (h + 1) * GROUP)
            ho_ref[own, p] = mm(pb[r], v[:, p]).astype(BF)
            gq_ref[own, p] = mm(gs[r], k[:, p]).astype(BF)
            gk.append(mm_tn(gs[r], q[:, p]).astype(BF))
            gv.append(mm_tn(pb[r], gh[:, p]).astype(BF))
        gk = jnp.concatenate(gk, axis=1)
        gv = jnp.concatenate(gv, axis=1)
        slot = g % 2
        grad[slot] = mm_nt(gk, wk_ref[...]) + mm_nt(gv, wv_ref[...])
        for step in range(XS):
            for out, base in ((keep_ref, 8), (send_ref, 8 + XS)):
                at = pl.ds(pl.multiple_of(index_ref[base + step] * cols, cols), cols)
                out[step, two] = grad[slot, :, at].astype(BF).reshape(NBR, depth, cols)


def attend(indices, pieces, q, gh, w_key, w_value, first):
    neigh, depth, cols = pieces[0].shape
    length, width = 2 * q[0].shape[0], q[0].shape[1]
    rows = neigh // NBR * GROUP
    small = jax.ShapeDtypeStruct((rows, width), BF)
    half = jax.ShapeDtypeStruct((XS, neigh, depth, cols), BF)
    return pl.pallas_call(
        functools.partial(attend_kernel, first=first),
        in_specs=[SMEM] + [ANY] * 14,
        out_specs=[VMEM] * 4,
        scratch_shapes=[
            pltpu.VMEM((neigh, depth, 8 * cols), BF),
            pltpu.VMEM((length, width), BF),
            pltpu.VMEM((length, width), BF),
            pltpu.VMEM(w_key.shape, BF),
            pltpu.VMEM(w_value.shape, BF),
            pltpu.VMEM((2, NBR * depth, 8 * cols), F32),
            pltpu.SemaphoreType.DMA((18 + 8 * neigh // NBR,)),
        ],
        out_shape=[small, small, half, half],
        compiler_params=params(BIG),
        cost_estimate=cost(8 * neigh * depth * 8 * cols * width, 6 << 20),
        name="attend",
    )(indices, *pieces, *q, *gh, w_key, w_value)


def halves_kernel(index_ref, *refs, chunks):
    rows_ref, (mine_ref, theirs_ref) = refs[: 2 * chunks], refs[2 * chunks : 2 * chunks + 2]
    all_ref = refs[-1]
    rows = mine_ref.shape[1] // XS
    for i in range(2):
        at = 0
        for src in rows_ref[i * chunks : (i + 1) * chunks]:
            all_ref[at : at + src.shape[0], :] = src[...]
            at += src.shape[0]
        for out, base in ((mine_ref, 8), (theirs_ref, 8 + XS)):
            for j in range(XS):
                at = pl.ds(pl.multiple_of(index_ref[base + j] * rows, 16), rows)
                out[i, j * rows : (j + 1) * rows, :] = all_ref[at, :]


def halves(indices, gq, ho):
    chunks = len(gq)
    length, width = sum(a.shape[0] for a in gq), gq[0].shape[1]
    out = jax.ShapeDtypeStruct((2, length // 2, width), BF)
    return pl.pallas_call(
        functools.partial(halves_kernel, chunks=chunks),
        in_specs=[SMEM] + [VMEM] * (2 * chunks),
        out_specs=[VMEM] * 2,
        scratch_shapes=[pltpu.VMEM((length, width), BF)],
        out_shape=[out, out],
        compiler_params=params(8),
        cost_estimate=cost(0, 1 << 20),
        name="halves",
    )(indices, *gq, *ho)


def outs_kernel(mine_ref, got_ref, wq_any, wqx_any, wo_any, wox_any, *refs, cut):
    out_refs, (wq_ref, wqx_ref, wo_ref, wox_ref, sems) = refs[:XS], refs[XS:]
    rows = mine_ref.shape[1] // XS
    steps = wq_ref.shape[0] // cut
    copies = []
    for k in range(steps):
        part = pl.ds(k * cut, cut)
        moves = [(wq_any.at[part, :], wq_ref.at[part, :]), (wqx_any.at[part, :], wqx_ref.at[part, :])]
        moves += [(wo_any.at[:, part], wo_ref.at[:, part]), (wox_any.at[:, part], wox_ref.at[:, part])]
        copies.append(
            [pltpu.make_async_copy(s, d, sems.at[4 * k + i]) for i, (s, d) in enumerate(moves)]
        )
        for copy in copies[-1]:
            copy.start()
    for k in range(steps):
        for copy in copies[k]:
            copy.wait()
        part = slice(k * cut, (k + 1) * cut)
        gt = mm_nt(mine_ref[0], wq_ref[part, :]) + mm_nt(got_ref[0], wqx_ref[part, :])
        at = mm(mine_ref[1], wo_ref[:, part]) + mm(got_ref[1], wox_ref[:, part])
        for i, r in enumerate((gt, at)):
            for j in range(XS):
                out_refs[j][i, :, part] = r[j * rows : (j + 1) * rows].astype(BF)


def outs(mine, got, w_query, wx_query, w_out, wx_out):
    _, length, width = mine.shape
    full = w_query.shape[0]
    cut = full // 8
    return pl.pallas_call(
        functools.partial(outs_kernel, cut=cut),
        in_specs=[VMEM] * 2 + [ANY] * 4,
        out_specs=[VMEM] * XS,
        scratch_shapes=[
            pltpu.VMEM(w_query.shape, BF),
            pltpu.VMEM(w_query.shape, BF),
            pltpu.VMEM(w_out.shape, BF),
            pltpu.VMEM(w_out.shape, BF),
            pltpu.SemaphoreType.DMA((4 * (full // cut),)),
        ],
        out_shape=[jax.ShapeDtypeStruct((2, length // XS, full), BF)] * XS,
        compiler_params=params(BIG),
        cost_estimate=cost(int(OUTS * 8 * length * width * full), int(OUTS * (16 << 20))),
        name="outs",
    )(mine, got, w_query, wx_query, w_out, wx_out)


def pick_kernel(index_ref, table_ref, *out_refs):
    at = 0
    for out in out_refs:
        for i in range(out.shape[0]):
            out[i] = table_ref[index_ref[at]]
            at += 1


def pick(index, table, counts, name, block=None):
    spec = pl.BlockSpec(table.shape, lambda i, s: (0,) * table.ndim) if block is None else block
    rest = table.shape[1:] if block is None else block.block_shape[1:]
    return pl.pallas_call(
        pick_kernel,
        grid_spec=pltpu.PrefetchScalarGridSpec(
            num_scalar_prefetch=1,
            grid=(1,),
            in_specs=[spec],
            out_specs=[pl.BlockSpec((n, *rest), lambda i, s: (0, 0, 0)) for n in counts],
        ),
        out_shape=[jax.ShapeDtypeStruct((n, *rest), table.dtype) for n in counts],
        compiler_params=params(16),
        cost_estimate=cost(0, 2 << 20),
        name=name,
    )(index, table)


def place_kernel(place_ref, *refs):
    out_ref, total = refs[-2:]
    at = 0
    for i in range(0, len(refs) - 2, XS):
        n = refs[i].shape[0]
        acc = refs[i][...].astype(F32)
        for r in refs[i + 1 : i + XS]:
            acc = acc + r[...].astype(F32)
        total[at : at + n] = acc.astype(BF)
        at += n
    for i in range(out_ref.shape[0]):
        out_ref[i] = total[place_ref[i]]


def place_sums(place, parts):
    flat = [p for chunk in parts for p in chunk]
    rest = flat[0].shape[1:]
    neigh = sum(chunk[0].shape[0] for chunk in parts)
    return pl.pallas_call(
        place_kernel,
        grid_spec=pltpu.PrefetchScalarGridSpec(
            num_scalar_prefetch=1,
            grid=(1,),
            in_specs=[pl.BlockSpec(p.shape, lambda i, s: (0, 0, 0)) for p in flat],
            out_specs=pl.BlockSpec((place.shape[0], *rest), lambda i, s: (0, 0, 0)),
            scratch_shapes=[pltpu.VMEM((neigh, *rest), BF)],
        ),
        out_shape=jax.ShapeDtypeStruct((place.shape[0], *rest), BF),
        compiler_params=params(16),
        cost_estimate=cost(0, 4 << 20),
        name="place",
    )(place, *flat)


def collect_kernel(slot_ref, held_ref, in_ref, out_ref):
    out_ref[...] = jnp.zeros(out_ref.shape, F32)
    for i in range(in_ref.shape[0]):

        @pl.when(held_ref[i] > 0)
        def _():
            out_ref[slot_ref[i]] += in_ref[i].astype(F32)


def collect(slot, held, returned, count):
    rest = returned.shape[1:]
    return pl.pallas_call(
        collect_kernel,
        in_specs=[SMEM, SMEM, VMEM],
        out_specs=VMEM,
        out_shape=jax.ShapeDtypeStruct((count, *rest), F32),
        compiler_params=params(16),
        cost_estimate=cost(0, 2 << 20),
        name="collect",
    )(slot, held, returned)


def final_kernel(*refs):
    total = refs[0][...].astype(F32)
    for r in refs[1:XS]:
        total = total + r[...].astype(F32)
    total = total.astype(BF)
    refs[XS][...] = total[0]
    refs[XS + 1][...] = total[1]


def final_sums(parts):
    two, rows, full = parts[0].shape
    cut = 1024
    out = jax.ShapeDtypeStruct((rows, full), BF)
    return pl.pallas_call(
        final_kernel,
        grid=(full // cut,),
        in_specs=[pl.BlockSpec((two, rows, cut), lambda i: (0, 0, i))] * XS,
        out_specs=[pl.BlockSpec((rows, cut), lambda i: (0, i))] * 2,
        out_shape=[out, out],
        compiler_params=params(16),
        cost_estimate=cost(LAST << 20, 4 << 20),
        name="final",
    )(*parts)


def chip_sums(keep, got):
    return [(keep[i].astype(F32) + got[i].astype(F32)).astype(BF) for i in range(XS)]


def x_parts(sums):
    return sums[:1] + [lax.ppermute(sums[i], "mp", x_perm(i)) for i in range(1, XS)]


def body(
    tokens, encoded, neighbour_owner, neighbour_slot, w_query, w_key, w_value, w_out, grad_out
):
    dp_count = lax.axis_size("dp")
    dp_at = lax.axis_index("dp")
    mp_at = lax.axis_index("mp")
    x, c = mp_at // CORES, mp_at % CORES
    neigh = neighbour_owner.shape[1] * NBR
    share = encoded.shape[2] // (XS * CORES)
    owners = piece_owners(x, c)
    targets = jnp.stack(
        [2 * ((x + i) % XS) + c for i in range(XS)]
        + [2 * ((x + i) % XS) + 1 - c for i in range(XS)]
    ).astype(jnp.int32)
    indices = jnp.concatenate([owners, targets])

    owners_all = neighbour_owner.reshape(dp_count, neigh)
    slots_all = neighbour_slot.reshape(dp_count, neigh)
    held_here = owners_all == dp_at
    held = jnp.any(held_here, axis=1).astype(jnp.int32)
    held_slot = jnp.sum(jnp.where(held_here, slots_all, 0), axis=1).astype(jnp.int32)
    my_owners = lax.dynamic_index_in_dim(owners_all, dp_at, 0, keepdims=False)
    place = jnp.argmax(my_owners[None, :] == jnp.arange(dp_count)[:, None], axis=1).astype(
        jnp.int32
    )

    wx_query, wx_out = swap(w_query), swap(w_out)
    t_own = x_pieces(tokens)
    g_own = x_pieces(grad_out)
    column = pl.BlockSpec(
        (encoded.shape[0], encoded.shape[1], share), lambda i, s: (0, 0, s[dp_count])
    )
    (outgoing,) = pick(
        jnp.concatenate([held_slot, mp_at[None].astype(jnp.int32)]),
        encoded,
        [dp_count],
        "outgoing",
        column,
    )
    arrived = lax.all_to_all(outgoing, "dp", split_axis=0, concat_axis=0, tiled=True)
    q_own, q_send = project(t_own, w_query, wx_query, False, "query", FIRST)
    near = pick(
        my_owners, after(arrived, (q_own, g_own)), [neigh // CHUNKS] * CHUNKS, "nearby"
    )
    gh_own, gh_send = project(after(g_own, near), w_out, wx_out, True, "gheads")
    near = [x_pieces(part) for part in near]
    query, grad_heads = (q_own, swap(q_send)), (gh_own, swap(gh_send))
    ho, gq, parts = [], [], []
    for i in range(CHUNKS):
        own = after(near[i], gh_own)
        ho_i, gq_i, keep, send = attend(
            indices,
            own + [swap(piece) for piece in own],
            query,
            grad_heads,
            w_key,
            w_value,
            i * neigh // CHUNKS // NBR,
        )
        sums = chip_sums(keep, swap(send))
        parts.append(x_parts(sums))
        ho.append(ho_i)
        gq.append(gq_i)
        query = after(query, sums)
    mine, theirs = halves(indices, gq, ho)
    sums2 = list(
        outs(after(mine, sums), swap(theirs), w_query, wx_query, w_out, wx_out)
    )
    parts2 = x_parts(after(sums2, parts))
    parts = after(parts, sums2)
    returned = lax.all_to_all(
        place_sums(place, parts), "dp", split_axis=0, concat_axis=0, tiled=True
    )
    grad_tokens, attended = final_sums(parts2)
    grad_encoded = collect(held_slot, held, after(returned, attended), encoded.shape[0])
    return (attended, grad_tokens, grad_encoded)


def solution(mesh):
    placed = (
        P(("dp", "mp"), None),
        P("dp", None, None),
        P(),
        P(),
        P(None, "mp"),
        P(None, "mp"),
        P(None, "mp"),
        P("mp", None),
        P(("dp", "mp"), None),
    )
    return jax.shard_map(
        body,
        mesh=mesh,
        in_specs=placed,
        out_specs=(P(("dp", "mp"), None), P(("dp", "mp"), None), P("dp", None, "mp")),
        check_vma=False,
    )
```

```python
import functools
import math

import jax
import jax.numpy as jnp
from jax import lax
from jax.experimental import pallas as pl
from jax.experimental.pallas import tpu as pltpu
from jax.sharding import PartitionSpec as P

HD = 128
GROUP = 64
NBR = 2
XS = 4
CORES = 2
BF = jnp.bfloat16
F32 = jnp.float32
BIG = 56
B_PROJ = 56
B_ATT = 40
B_OUTS = 30
FIRST = 16
OUTS = 0.3
LAST = 65536
ATT = 1
NT = (((1,), (1,)), ((), ()))
TN = (((0,), (0,)), ((), ()))


def mm(a, b):
    return jnp.dot(a, b, preferred_element_type=F32)


def mm_nt(a, b):
    return lax.dot_general(a, b, NT, preferred_element_type=F32)


def mm_tn(a, b):
    return lax.dot_general(a, b, TN, preferred_element_type=F32)


def x_perm(step):
    return [(2 * x + c, 2 * ((x + step) % XS) + c) for x in range(XS) for c in range(CORES)]


CORE_SWAP = [(2 * x + c, 2 * x + 1 - c) for x in range(XS) for c in range(CORES)]


def x_pieces(block):
    return [block] + [lax.ppermute(block, "mp", x_perm(-i)) for i in range(1, XS)]


def swap(block):
    return lax.ppermute(block, "mp", CORE_SWAP)


def after(values, earlier):
    return lax.optimization_barrier((values, earlier))[0]


def by_distance(x, c):
    own = [2 * ((x + i) % XS) + c for i in range(XS)]
    other = [2 * ((x + i) % XS) + 1 - c for i in range(XS)]
    return jnp.stack(own + other).astype(jnp.int32)


ANY = pl.BlockSpec(memory_space=pl.ANY)
SMEM = pl.BlockSpec(memory_space=pltpu.SMEM)
VMEM = pl.BlockSpec(memory_space=pltpu.VMEM)


def params(mib):
    return pltpu.CompilerParams(vmem_limit_bytes=mib << 20)


def cost(flops, bytes_accessed):
    return pl.CostEstimate(flops=flops, bytes_accessed=bytes_accessed, transcendentals=0)


def project_kernel(*refs, cut, transposed):
    pieces = refs[:4]
    w_any, wx_any, out_ref, outx_ref, a_ref, w_ref, wx_ref, acc, accx, sems = refs[4:]
    rows = pieces[0].shape[0]
    steps = a_ref.shape[1] // cut
    copies = []
    for j, piece in enumerate(pieces):
        at = pl.ds(j * rows, rows)
        copies.append(pltpu.make_async_copy(piece, a_ref.at[at, :], sems.at[j]))
        copies[-1].start()

    def weights(k):
        part = pl.ds(pl.multiple_of(k * cut, cut), cut)
        at = (slice(None), part) if transposed else (part, slice(None))
        return [
            pltpu.make_async_copy(w_any.at[at], w_ref.at[at], sems.at[4 + 2 * k]),
            pltpu.make_async_copy(wx_any.at[at], wx_ref.at[at], sems.at[5 + 2 * k]),
        ]

    for k in range(steps):
        for copy in weights(k):
            copy.start()
    acc[...] = jnp.zeros(acc.shape, F32)
    accx[...] = jnp.zeros(accx.shape, F32)
    for copy in copies:
        copy.wait()

    def step(k, _):
        part = pl.ds(pl.multiple_of(k * cut, cut), cut)
        a = a_ref[:, part]
        for copy, w, total in zip(weights(k), (w_ref, wx_ref), (acc, accx)):
            copy.wait()
            total[...] += mm_nt(a, w[:, part]) if transposed else mm(a, w[part, :])
        return 0

    lax.fori_loop(0, steps, step, 0)
    out_ref[...] = acc[...].astype(BF)
    outx_ref[...] = accx[...].astype(BF)


def project(pieces, w, wx, transposed, name, weight=1):
    rows, depth = pieces[0].shape
    width = w.shape[0] if transposed else w.shape[1]
    length = rows * len(pieces)
    cut = depth // 8
    out = jax.ShapeDtypeStruct((length, width), BF)
    return pl.pallas_call(
        functools.partial(project_kernel, cut=cut, transposed=transposed),
        in_specs=[ANY] * 6,
        out_specs=[VMEM] * 2,
        scratch_shapes=[
            pltpu.VMEM((length, depth), BF),
            pltpu.VMEM(w.shape, BF),
            pltpu.VMEM(w.shape, BF),
            pltpu.VMEM((length, width), F32),
            pltpu.VMEM((length, width), F32),
            pltpu.SemaphoreType.DMA((4 + 2 * (depth // cut),)),
        ],
        out_shape=[out, out],
        compiler_params=params(B_PROJ),
        cost_estimate=cost(int(4 * length * depth * width * weight), 1 << 20),
        name=name,
    )(*pieces, w, wx)


def arrange_kernel(index_ref, wk_any, wv_any, wk_out, wv_out, sems):
    rows = wk_any.shape[0] // 8
    copies = []
    for j in range(8):
        at = pl.ds(pl.multiple_of(index_ref[j] * rows, rows), rows)
        put = pl.ds(j * rows, rows)
        for i, (w, o) in enumerate(((wk_any, wk_out), (wv_any, wv_out))):
            copies.append(pltpu.make_async_copy(w.at[at, :], o.at[put, :], sems.at[2 * j + i]))
            copies[-1].start()
    for copy in copies:
        copy.wait()


def arrange(indices, w_key, w_value):
    out = jax.ShapeDtypeStruct(w_key.shape, BF)
    return pl.pallas_call(
        arrange_kernel,
        in_specs=[SMEM, ANY, ANY],
        out_specs=[ANY] * 2,
        scratch_shapes=[pltpu.SemaphoreType.DMA((16,))],
        out_shape=[out, out],
        compiler_params=params(8),
        cost_estimate=cost(0, 1 << 20),
        name="arrange",
    )(indices, w_key, w_value)


def assemble_kernel(index_ref, *refs):
    parts, outs_ref = refs[:4], refs[4:]
    rows = outs_ref[0].shape[0] // 8
    for i in range(2):
        for j in range(8):
            at = pl.ds(pl.multiple_of(index_ref[j] * rows, 16), rows)
            part = slice(j % XS * rows, (j % XS + 1) * rows)
            outs_ref[i][at, :] = parts[2 * i + j // XS][part, :]


def assemble(indices, q, gh):
    out = jax.ShapeDtypeStruct((2 * q[0].shape[0], q[0].shape[1]), BF)
    return pl.pallas_call(
        assemble_kernel,
        in_specs=[SMEM] + [VMEM] * 4,
        out_specs=[VMEM] * 2,
        out_shape=[out, out],
        compiler_params=params(8),
        cost_estimate=cost(0, 1 << 20),
        name="assemble",
    )(indices, *q, *gh)


def attend_kernel(index_ref, *refs):
    pieces = refs[:8]
    q_any, gh_any, wk_any, wv_any, mine_any, theirs_any, keep_any, send_any = refs[8:16]
    near, q_ref, gh_ref, wk_ref, wv_ref, small, share, sems, out_sems = refs[16:]
    neigh, depth, _ = near.shape
    cols = pieces[0].shape[2]
    groups = neigh // NBR
    keys = NBR * depth
    heads = q_ref.shape[1] // HD
    scale = 1.0 / math.sqrt(HD)
    moves = [(wk_any, wk_ref)]
    for j in range(8):
        part = pl.ds(0, NBR)
        moves.append((pieces[j].at[part], near.at[part, :, pl.ds(j * cols, cols)]))
    moves += [(wv_any, wv_ref), (q_any, q_ref), (gh_any, gh_ref)]
    head = len(moves)
    later = pl.ds(NBR, neigh - NBR)
    for j in range(8):
        moves.append((pieces[j].at[later], near.at[later, :, pl.ds(j * cols, cols)]))
    copies = [pltpu.make_async_copy(s, d, sems.at[i]) for i, (s, d) in enumerate(moves)]
    for copy in copies:
        copy.start()
    part = [slice(h * HD, (h + 1) * HD) for h in range(heads)]

    def stores(g):
        two = pl.ds(g * NBR, NBR)
        return [
            pltpu.make_async_copy(share.at[pl.ds(0, XS), two], keep_any.at[:, two], out_sems.at[2 * g]),
            pltpu.make_async_copy(share.at[pl.ds(XS, XS), two], send_any.at[:, two], out_sems.at[2 * g + 1]),
        ]

    def group(g, _):
        own = pl.ds(pl.multiple_of(g * GROUP, GROUP), GROUP)
        two = pl.ds(g * NBR, NBR)

        @pl.when(g == 1)
        def _():
            for copy in copies[head:]:
                copy.wait()

        near_rows = near[two].reshape(keys, near.shape[2])
        k = mm(near_rows, wk_ref[...]).astype(BF)
        v = mm(near_rows, wv_ref[...]).astype(BF)
        q = q_ref[own, :]
        gh = gh_ref[own, :]
        s = jnp.concatenate([mm_nt(q[:, p], k[:, p]) for p in part], axis=0) * scale
        gp = jnp.concatenate([mm_nt(gh[:, p], v[:, p]) for p in part], axis=0)
        e = jnp.exp(s - jnp.max(s, axis=-1, keepdims=True))
        probs = e * (1.0 / jnp.sum(e, axis=-1, keepdims=True))
        pb = probs.astype(BF)
        centre = jnp.sum(probs * gp, axis=-1, keepdims=True)
        gs = (probs * (gp - centre) * scale).astype(BF)
        gk = []
        gv = []
        for h, p in enumerate(part):
            r = slice(h * GROUP, (h + 1) * GROUP)
            small[0, own, p] = mm(pb[r], v[:, p]).astype(BF)
            small[1, own, p] = mm(gs[r], k[:, p]).astype(BF)
            gk.append(mm_tn(gs[r], q[:, p]).astype(BF))
            gv.append(mm_tn(pb[r], gh[:, p]).astype(BF))
        gk = jnp.concatenate(gk, axis=1)
        gv = jnp.concatenate(gv, axis=1)
        for j in range(0, 8, 2):
            put = slice(j * cols, (j + 2) * cols)
            grad = (mm_nt(gk, wk_ref[put, :]) + mm_nt(gv, wv_ref[put, :])).astype(BF)
            share[j, two] = grad[:, :cols].reshape(NBR, depth, cols)
            share[j + 1, two] = grad[:, cols:].reshape(NBR, depth, cols)
        for copy in stores(g):
            copy.start()
        return 0

    for copy in copies[:head]:
        copy.wait()
    lax.fori_loop(0, groups, group, 0)
    rows = small.shape[1] // 8
    last = []
    for j in range(8):
        at = pl.ds(pl.multiple_of(index_ref[j] * rows, 16), rows)
        put = pl.ds(j % XS * rows, rows)
        dst = (mine_any, theirs_any)[j // XS].at[:, put, :]
        last.append(pltpu.make_async_copy(small.at[:, at, :], dst, out_sems.at[2 * groups + j]))
        last[-1].start()
    for g in range(groups):
        for copy in stores(g):
            copy.wait()
    for copy in last:
        copy.wait()


def attend(indices, pieces, q, gh, w_key, w_value):
    neigh, depth, cols = pieces[0].shape
    length, width = q.shape
    groups = neigh // NBR
    share = jax.ShapeDtypeStruct((XS, neigh, depth, cols), BF)
    half = jax.ShapeDtypeStruct((2, length // 2, width), BF)
    return pl.pallas_call(
        attend_kernel,
        in_specs=[SMEM] + [ANY] * 12,
        out_specs=[ANY] * 4,
        scratch_shapes=[
            pltpu.VMEM((neigh, depth, 8 * cols), BF),
            pltpu.VMEM((length, width), BF),
            pltpu.VMEM((length, width), BF),
            pltpu.VMEM(w_key.shape, BF),
            pltpu.VMEM(w_value.shape, BF),
            pltpu.VMEM((2, length, width), BF),
            pltpu.VMEM((8, neigh, depth, cols), BF),
            pltpu.SemaphoreType.DMA((20,)),
            pltpu.SemaphoreType.DMA((2 * groups + 8,)),
        ],
        out_shape=[half, half, share, share],
        compiler_params=params(B_ATT),
        cost_estimate=cost(int(ATT * 8 * neigh * depth * 8 * cols * width), 1 << 20),
        name="attend",
    )(indices, *pieces, q, gh, w_key, w_value)


def outs_kernel(mine_any, got_any, wq_any, wqx_any, wo_any, wox_any, *refs, cut):
    out_refs, (mine_ref, got_ref, wq_ref, wqx_ref, wo_ref, wox_ref, sems) = refs[:XS], refs[XS:]
    rows = mine_ref.shape[1] // XS
    steps = wq_ref.shape[0] // cut
    first = [
        pltpu.make_async_copy(mine_any, mine_ref, sems.at[4 * steps]),
        pltpu.make_async_copy(got_any, got_ref, sems.at[4 * steps + 1]),
    ]

    def weights(k):
        part = pl.ds(pl.multiple_of(k * cut, cut), cut)
        moves = [(w.at[part, :], r.at[part, :]) for w, r in ((wq_any, wq_ref), (wqx_any, wqx_ref))]
        moves += [(w.at[:, part], r.at[:, part]) for w, r in ((wo_any, wo_ref), (wox_any, wox_ref))]
        return [pltpu.make_async_copy(s, d, sems.at[4 * k + i]) for i, (s, d) in enumerate(moves)]

    for copy in first:
        copy.start()
    for k in range(steps):
        for copy in weights(k):
            copy.start()
    for copy in first:
        copy.wait()

    def step(k, _):
        for copy in weights(k):
            copy.wait()
        part = pl.ds(pl.multiple_of(k * cut, cut), cut)
        gt = mm_nt(mine_ref[1], wq_ref[part, :]) + mm_nt(got_ref[1], wqx_ref[part, :])
        at = mm(mine_ref[0], wo_ref[:, part]) + mm(got_ref[0], wox_ref[:, part])
        for i, r in enumerate((gt, at)):
            for j in range(XS):
                out_refs[j][i, :, part] = r[j * rows : (j + 1) * rows].astype(BF)
        return 0

    lax.fori_loop(0, steps, step, 0)


def outs(mine, got, w_query, wx_query, w_out, wx_out):
    _, length, width = mine.shape
    full = w_query.shape[0]
    cut = full // 8
    return pl.pallas_call(
        functools.partial(outs_kernel, cut=cut),
        in_specs=[ANY] * 6,
        out_specs=[VMEM] * XS,
        scratch_shapes=[
            pltpu.VMEM(mine.shape, BF),
            pltpu.VMEM(mine.shape, BF),
            pltpu.VMEM(w_query.shape, BF),
            pltpu.VMEM(w_query.shape, BF),
            pltpu.VMEM(w_out.shape, BF),
            pltpu.VMEM(w_out.shape, BF),
            pltpu.SemaphoreType.DMA((4 * (full // cut) + 2,)),
        ],
        out_shape=[jax.ShapeDtypeStruct((2, length // XS, full), BF)] * XS,
        compiler_params=params(B_OUTS),
        cost_estimate=cost(int(OUTS * 8 * length * width * full), int(OUTS * (16 << 20))),
        name="outs",
    )(mine, got, w_query, wx_query, w_out, wx_out)


def pick_kernel(index_ref, table_ref, *out_refs):
    at = 0
    for out in out_refs:
        for i in range(out.shape[0]):
            out[i] = table_ref[index_ref[at]]
            at += 1


def pick(index, table, counts, name):
    rest = table.shape[1:]
    return pl.pallas_call(
        pick_kernel,
        in_specs=[SMEM, VMEM],
        out_specs=[VMEM] * len(counts),
        out_shape=[jax.ShapeDtypeStruct((n, *rest), table.dtype) for n in counts],
        compiler_params=params(16),
        cost_estimate=cost(0, 1 << 20),
        name=name,
    )(index, table)


def outgoing_kernel(slot_ref, at_ref, table_any, out_ref, part, sem):
    cols = out_ref.shape[2]
    at = pl.ds(pl.multiple_of(at_ref[0] * cols, cols), cols)
    copy = pltpu.make_async_copy(table_any.at[:, :, at], part, sem)
    copy.start()
    copy.wait()
    for i in range(out_ref.shape[0]):
        out_ref[i] = part[slot_ref[i]]


def choose_outgoing(slot, at, table, cols):
    count, depth, _ = table.shape
    return pl.pallas_call(
        outgoing_kernel,
        in_specs=[SMEM, SMEM, ANY],
        out_specs=VMEM,
        scratch_shapes=[pltpu.VMEM((count, depth, cols), BF), pltpu.SemaphoreType.DMA(())],
        out_shape=jax.ShapeDtypeStruct((slot.shape[0], depth, cols), BF),
        compiler_params=params(BIG),
        cost_estimate=cost(0, 1 << 20),
        name="outgoing",
    )(slot, at, table)


def place_kernel(place_ref, *refs):
    out_ref, total = refs[-2:]
    at = 0
    for i in range(0, len(refs) - 2, XS):
        n = refs[i].shape[0]
        acc = refs[i][...].astype(F32)
        for r in refs[i + 1 : i + XS]:
            acc = acc + r[...].astype(F32)
        total[at : at + n] = acc.astype(BF)
        at += n
    for i in range(out_ref.shape[0]):
        out_ref[i] = total[place_ref[i]]


def place_sums(place, parts):
    flat = [p for chunk in parts for p in chunk]
    rest = flat[0].shape[1:]
    neigh = sum(chunk[0].shape[0] for chunk in parts)
    return pl.pallas_call(
        place_kernel,
        grid_spec=pltpu.PrefetchScalarGridSpec(
            num_scalar_prefetch=1,
            grid=(1,),
            in_specs=[pl.BlockSpec(p.shape, lambda i, s: (0, 0, 0)) for p in flat],
            out_specs=pl.BlockSpec((place.shape[0], *rest), lambda i, s: (0, 0, 0)),
            scratch_shapes=[pltpu.VMEM((neigh, *rest), BF)],
        ),
        out_shape=jax.ShapeDtypeStruct((place.shape[0], *rest), BF),
        compiler_params=params(16),
        cost_estimate=cost(0, 4 << 20),
        name="place",
    )(place, *flat)


def collect_kernel(slot_ref, held_ref, in_ref, out_ref):
    out_ref[...] = jnp.zeros(out_ref.shape, F32)
    for i in range(in_ref.shape[0]):

        @pl.when(held_ref[i] > 0)
        def _():
            out_ref[slot_ref[i]] += in_ref[i].astype(F32)


def collect(slot, held, returned, count):
    rest = returned.shape[1:]
    return pl.pallas_call(
        collect_kernel,
        in_specs=[SMEM, SMEM, VMEM],
        out_specs=VMEM,
        out_shape=jax.ShapeDtypeStruct((count, *rest), F32),
        compiler_params=params(16),
        cost_estimate=cost(0, 2 << 20),
        name="collect",
    )(slot, held, returned)


def final_kernel(*refs):
    total = refs[0][...].astype(F32)
    for r in refs[1:XS]:
        total = total + r[...].astype(F32)
    total = total.astype(BF)
    refs[XS][...] = total[0]
    refs[XS + 1][...] = total[1]


def final_sums(parts):
    two, rows, full = parts[0].shape
    cut = 1024
    out = jax.ShapeDtypeStruct((rows, full), BF)
    return pl.pallas_call(
        final_kernel,
        grid=(full // cut,),
        in_specs=[pl.BlockSpec((two, rows, cut), lambda i: (0, 0, i))] * XS,
        out_specs=[pl.BlockSpec((rows, cut), lambda i: (0, i))] * 2,
        out_shape=[out, out],
        compiler_params=params(16),
        cost_estimate=cost(LAST << 20, 4 << 20),
        name="final",
    )(*parts)


def chip_sums(keep, got):
    return [(keep[i].astype(F32) + got[i].astype(F32)).astype(BF) for i in range(XS)]


def x_parts(sums):
    return sums[:1] + [lax.ppermute(sums[i], "mp", x_perm(i)) for i in range(1, XS)]


def body(
    tokens, encoded, neighbour_owner, neighbour_slot, w_query, w_key, w_value, w_out, grad_out
):
    dp_count = lax.axis_size("dp")
    dp_at = lax.axis_index("dp")
    mp_at = lax.axis_index("mp")
    x, c = mp_at // CORES, mp_at % CORES
    neigh = neighbour_owner.shape[1] * NBR
    share = encoded.shape[2] // (XS * CORES)
    indices = by_distance(x, c)

    owners_all = neighbour_owner.reshape(dp_count, neigh)
    slots_all = neighbour_slot.reshape(dp_count, neigh)
    held_here = owners_all == dp_at
    held = jnp.any(held_here, axis=1).astype(jnp.int32)
    held_slot = jnp.sum(jnp.where(held_here, slots_all, 0), axis=1).astype(jnp.int32)
    my_owners = lax.dynamic_index_in_dim(owners_all, dp_at, 0, keepdims=False)
    place = jnp.argmax(my_owners[None, :] == jnp.arange(dp_count)[:, None], axis=1).astype(
        jnp.int32
    )

    t_own = x_pieces(tokens)
    g_own = x_pieces(grad_out)
    outgoing = choose_outgoing(held_slot, mp_at[None].astype(jnp.int32), encoded, share)
    arrived = lax.all_to_all(outgoing, "dp", split_axis=0, concat_axis=0, tiled=True)
    wx_query, wx_out = swap(w_query), swap(w_out)
    q_own, q_send = project(
        t_own, w_query, wx_query, False, "query", FIRST
    )
    q_got = swap(q_send)
    w_key, w_value = arrange(indices, after(w_key, q_own), w_value)
    (near,) = pick(my_owners, after(arrived, (q_own, q_got, g_own, w_key)), [neigh], "nearby")
    gh_own, gh_send = project(after(g_own, near), w_out, wx_out, True, "gheads", 0)
    near = x_pieces(near)
    gh_got = swap(gh_send)
    query, grad_heads = assemble(indices, (q_own, q_got), (gh_own, gh_got))
    own = [after(piece, grad_heads) for piece in near]
    pieces = own + [swap(piece) for piece in own]
    mine, theirs, keep, send = attend(indices, pieces, query, grad_heads, w_key, w_value)
    sums = chip_sums(keep, swap(send))
    parts = [x_parts(sums)]
    sums2 = list(
        outs(after(mine, sums), swap(theirs), w_query, wx_query, w_out, wx_out)
    )
    parts2 = x_parts(after(sums2, parts))
    parts = after(parts, sums2)
    returned = lax.all_to_all(
        place_sums(place, parts), "dp", split_axis=0, concat_axis=0, tiled=True
    )
    grad_tokens, attended = final_sums(parts2)
    grad_encoded = collect(held_slot, held, after(returned, attended), encoded.shape[0])
    return (attended, grad_tokens, grad_encoded)


def solution(mesh):
    placed = (
        P(("dp", "mp"), None),
        P("dp", None, None),
        P(),
        P(),
        P(None, "mp"),
        P(None, "mp"),
        P(None, "mp"),
        P("mp", None),
        P(("dp", "mp"), None),
    )
    return jax.shard_map(
        body,
        mesh=mesh,
        in_specs=placed,
        out_specs=(P(("dp", "mp"), None), P(("dp", "mp"), None), P("dp", None, "mp")),
        check_vma=False,
    )
```

```python
import functools
import math

import jax
import jax.numpy as jnp
from jax import lax
from jax.experimental import pallas as pl
from jax.experimental.pallas import tpu as pltpu
from jax.sharding import PartitionSpec as P

HD = 128
GROUP = 64
NBR = 2
XS = 4
CORES = 2
BF = jnp.bfloat16
F32 = jnp.float32
BIG = 56
B_PROJ = 56
B_ATT = 40
B_OUTS = 30
FIRST = 16
OUTS = 0.3
LAST = 65536
ATT = 1
NT = (((1,), (1,)), ((), ()))
TN = (((0,), (0,)), ((), ()))


def mm(a, b):
    return jnp.dot(a, b, preferred_element_type=F32)


def mm_nt(a, b):
    return lax.dot_general(a, b, NT, preferred_element_type=F32)


def mm_tn(a, b):
    return lax.dot_general(a, b, TN, preferred_element_type=F32)


def x_perm(step):
    return [(2 * x + c, 2 * ((x + step) % XS) + c) for x in range(XS) for c in range(CORES)]


CORE_SWAP = [(2 * x + c, 2 * x + 1 - c) for x in range(XS) for c in range(CORES)]


def x_pieces(block):
    return [block] + [lax.ppermute(block, "mp", x_perm(-i)) for i in range(1, XS)]


def swap(block):
    return lax.ppermute(block, "mp", CORE_SWAP)


def after(values, earlier):
    return lax.optimization_barrier((values, earlier))[0]


def by_distance(x, c):
    own = [2 * ((x + i) % XS) + c for i in range(XS)]
    other = [2 * ((x + i) % XS) + 1 - c for i in range(XS)]
    return jnp.stack(own + other).astype(jnp.int32)


ANY = pl.BlockSpec(memory_space=pl.ANY)
SMEM = pl.BlockSpec(memory_space=pltpu.SMEM)
VMEM = pl.BlockSpec(memory_space=pltpu.VMEM)


def params(mib):
    return pltpu.CompilerParams(vmem_limit_bytes=mib << 20)


def cost(flops, bytes_accessed):
    return pl.CostEstimate(flops=flops, bytes_accessed=bytes_accessed, transcendentals=0)


def project_kernel(*refs, cut, transposed):
    pieces = refs[:4]
    w_any, wx_any, out_ref, outx_ref, a_ref, w_ref, wx_ref, acc, accx, sems = refs[4:]
    rows = pieces[0].shape[0]
    steps = a_ref.shape[1] // cut
    copies = []
    for j, piece in enumerate(pieces):
        at = pl.ds(j * rows, rows)
        copies.append(pltpu.make_async_copy(piece, a_ref.at[at, :], sems.at[j]))
        copies[-1].start()

    def weights(k):
        part = pl.ds(pl.multiple_of(k * cut, cut), cut)
        at = (slice(None), part) if transposed else (part, slice(None))
        return [
            pltpu.make_async_copy(w_any.at[at], w_ref.at[at], sems.at[4 + 2 * k]),
            pltpu.make_async_copy(wx_any.at[at], wx_ref.at[at], sems.at[5 + 2 * k]),
        ]

    for k in range(steps):
        for copy in weights(k):
            copy.start()
    acc[...] = jnp.zeros(acc.shape, F32)
    accx[...] = jnp.zeros(accx.shape, F32)
    for copy in copies:
        copy.wait()

    def step(k, _):
        part = pl.ds(pl.multiple_of(k * cut, cut), cut)
        a = a_ref[:, part]
        for copy, w, total in zip(weights(k), (w_ref, wx_ref), (acc, accx)):
            copy.wait()
            total[...] += mm_nt(a, w[:, part]) if transposed else mm(a, w[part, :])
        return 0

    lax.fori_loop(0, steps, step, 0)
    out_ref[...] = acc[...].astype(BF)
    outx_ref[...] = accx[...].astype(BF)


def project(pieces, w, wx, transposed, name, weight=1):
    rows, depth = pieces[0].shape
    width = w.shape[0] if transposed else w.shape[1]
    length = rows * len(pieces)
    cut = depth // 8
    out = jax.ShapeDtypeStruct((length, width), BF)
    return pl.pallas_call(
        functools.partial(project_kernel, cut=cut, transposed=transposed),
        in_specs=[ANY] * 6,
        out_specs=[VMEM] * 2,
        scratch_shapes=[
            pltpu.VMEM((length, depth), BF),
            pltpu.VMEM(w.shape, BF),
            pltpu.VMEM(w.shape, BF),
            pltpu.VMEM((length, width), F32),
            pltpu.VMEM((length, width), F32),
            pltpu.SemaphoreType.DMA((4 + 2 * (depth // cut),)),
        ],
        out_shape=[out, out],
        compiler_params=params(B_PROJ),
        cost_estimate=cost(int(4 * length * depth * width * weight), 1 << 20),
        name=name,
    )(*pieces, w, wx)


def arrange_kernel(index_ref, wk_any, wv_any, wk_out, wv_out, sems):
    rows = wk_any.shape[0] // 8
    copies = []
    for j in range(8):
        at = pl.ds(pl.multiple_of(index_ref[j] * rows, rows), rows)
        put = pl.ds(j * rows, rows)
        for i, (w, o) in enumerate(((wk_any, wk_out), (wv_any, wv_out))):
            copies.append(pltpu.make_async_copy(w.at[at, :], o.at[put, :], sems.at[2 * j + i]))
            copies[-1].start()
    for copy in copies:
        copy.wait()


def arrange(indices, w_key, w_value):
    out = jax.ShapeDtypeStruct(w_key.shape, BF)
    return pl.pallas_call(
        arrange_kernel,
        in_specs=[SMEM, ANY, ANY],
        out_specs=[ANY] * 2,
        scratch_shapes=[pltpu.SemaphoreType.DMA((16,))],
        out_shape=[out, out],
        compiler_params=params(8),
        cost_estimate=cost(0, 1 << 20),
        name="arrange",
    )(indices, w_key, w_value)


def assemble_kernel(index_ref, *refs):
    parts, outs_ref = refs[:4], refs[4:]
    rows = outs_ref[0].shape[0] // 8
    for i in range(2):
        for j in range(8):
            at = pl.ds(pl.multiple_of(index_ref[j] * rows, 16), rows)
            part = slice(j % XS * rows, (j % XS + 1) * rows)
            outs_ref[i][at, :] = parts[2 * i + j // XS][part, :]


def assemble(indices, q, gh):
    out = jax.ShapeDtypeStruct((2 * q[0].shape[0], q[0].shape[1]), BF)
    return pl.pallas_call(
        assemble_kernel,
        in_specs=[SMEM] + [VMEM] * 4,
        out_specs=[VMEM] * 2,
        out_shape=[out, out],
        compiler_params=params(8),
        cost_estimate=cost(0, 1 << 20),
        name="assemble",
    )(indices, *q, *gh)


def attend_kernel(index_ref, *refs):
    pieces = refs[:8]
    q_ref, gh_ref, wk_ref, wv_ref, mine_any, theirs_any, keep_any, send_any = refs[8:16]
    near, small, share, sems, out_sems = refs[16:]
    neigh, depth, _ = near.shape
    cols = pieces[0].shape[2]
    groups = neigh // NBR
    keys = NBR * depth
    heads = q_ref.shape[1] // HD
    scale = 1.0 / math.sqrt(HD)
    moves = []
    for j in range(8):
        part = pl.ds(0, NBR)
        moves.append((pieces[j].at[part], near.at[part, :, pl.ds(j * cols, cols)]))
    head = len(moves)
    later = pl.ds(NBR, neigh - NBR)
    for j in range(8):
        moves.append((pieces[j].at[later], near.at[later, :, pl.ds(j * cols, cols)]))
    copies = [pltpu.make_async_copy(s, d, sems.at[i]) for i, (s, d) in enumerate(moves)]
    for copy in copies:
        copy.start()
    part = [slice(h * HD, (h + 1) * HD) for h in range(heads)]

    def stores(g):
        two = pl.ds(g * NBR, NBR)
        return [
            pltpu.make_async_copy(share.at[pl.ds(0, XS), two], keep_any.at[:, two], out_sems.at[2 * g]),
            pltpu.make_async_copy(share.at[pl.ds(XS, XS), two], send_any.at[:, two], out_sems.at[2 * g + 1]),
        ]

    def group(g, _):
        own = pl.ds(pl.multiple_of(g * GROUP, GROUP), GROUP)
        two = pl.ds(g * NBR, NBR)

        @pl.when(g == 1)
        def _():
            for copy in copies[head:]:
                copy.wait()

        near_rows = near[two].reshape(keys, near.shape[2])
        k = mm(near_rows, wk_ref[...]).astype(BF)
        v = mm(near_rows, wv_ref[...]).astype(BF)
        q = q_ref[own, :]
        gh = gh_ref[own, :]
        s = jnp.concatenate([mm_nt(q[:, p], k[:, p]) for p in part], axis=0) * scale
        gp = jnp.concatenate([mm_nt(gh[:, p], v[:, p]) for p in part], axis=0)
        e = jnp.exp(s - jnp.max(s, axis=-1, keepdims=True))
        probs = e * (1.0 / jnp.sum(e, axis=-1, keepdims=True))
        pb = probs.astype(BF)
        centre = jnp.sum(probs * gp, axis=-1, keepdims=True)
        gs = (probs * (gp - centre) * scale).astype(BF)
        gk = []
        gv = []
        for h, p in enumerate(part):
            r = slice(h * GROUP, (h + 1) * GROUP)
            small[0, own, p] = mm(pb[r], v[:, p]).astype(BF)
            small[1, own, p] = mm(gs[r], k[:, p]).astype(BF)
            gk.append(mm_tn(gs[r], q[:, p]).astype(BF))
            gv.append(mm_tn(pb[r], gh[:, p]).astype(BF))
        gk = jnp.concatenate(gk, axis=1)
        gv = jnp.concatenate(gv, axis=1)
        for j in range(0, 8, 2):
            put = slice(j * cols, (j + 2) * cols)
            grad = (mm_nt(gk, wk_ref[put, :]) + mm_nt(gv, wv_ref[put, :])).astype(BF)
            share[j, two] = grad[:, :cols].reshape(NBR, depth, cols)
            share[j + 1, two] = grad[:, cols:].reshape(NBR, depth, cols)
        for copy in stores(g):
            copy.start()
        return 0

    for copy in copies[:head]:
        copy.wait()
    lax.fori_loop(0, groups, group, 0)
    rows = small.shape[1] // 8
    last = []
    for j in range(8):
        at = pl.ds(pl.multiple_of(index_ref[j] * rows, 16), rows)
        put = pl.ds(j % XS * rows, rows)
        dst = (mine_any, theirs_any)[j // XS].at[:, put, :]
        last.append(pltpu.make_async_copy(small.at[:, at, :], dst, out_sems.at[2 * groups + j]))
        last[-1].start()
    for g in range(groups):
        for copy in stores(g):
            copy.wait()
    for copy in last:
        copy.wait()


def attend(indices, pieces, q, gh, w_key, w_value):
    neigh, depth, cols = pieces[0].shape
    length, width = q.shape
    groups = neigh // NBR
    share = jax.ShapeDtypeStruct((XS, neigh, depth, cols), BF)
    half = jax.ShapeDtypeStruct((2, length // 2, width), BF)
    return pl.pallas_call(
        attend_kernel,
        in_specs=[SMEM] + [ANY] * 8 + [VMEM] * 4,
        out_specs=[ANY] * 4,
        scratch_shapes=[
            pltpu.VMEM((neigh, depth, 8 * cols), BF),
            pltpu.VMEM((2, length, width), BF),
            pltpu.VMEM((8, neigh, depth, cols), BF),
            pltpu.SemaphoreType.DMA((20,)),
            pltpu.SemaphoreType.DMA((2 * groups + 8,)),
        ],
        out_shape=[half, half, share, share],
        compiler_params=params(B_ATT),
        cost_estimate=cost(int(ATT * 8 * neigh * depth * 8 * cols * width), 1 << 20),
        name="attend",
    )(indices, *pieces, q, gh, w_key, w_value)


def outs_kernel(mine_any, got_any, wq_any, wqx_any, wo_any, wox_any, *refs, cut):
    out_refs, (mine_ref, got_ref, wq_ref, wqx_ref, wo_ref, wox_ref, sems) = refs[:XS], refs[XS:]
    rows = mine_ref.shape[1] // XS
    steps = wq_ref.shape[0] // cut
    first = [
        pltpu.make_async_copy(mine_any, mine_ref, sems.at[4 * steps]),
        pltpu.make_async_copy(got_any, got_ref, sems.at[4 * steps + 1]),
    ]

    def weights(k):
        part = pl.ds(pl.multiple_of(k * cut, cut), cut)
        moves = [(w.at[part, :], r.at[part, :]) for w, r in ((wq_any, wq_ref), (wqx_any, wqx_ref))]
        moves += [(w.at[:, part], r.at[:, part]) for w, r in ((wo_any, wo_ref), (wox_any, wox_ref))]
        return [pltpu.make_async_copy(s, d, sems.at[4 * k + i]) for i, (s, d) in enumerate(moves)]

    for copy in first:
        copy.start()
    for k in range(steps):
        for copy in weights(k):
            copy.start()
    for copy in first:
        copy.wait()

    def step(k, _):
        for copy in weights(k):
            copy.wait()
        part = pl.ds(pl.multiple_of(k * cut, cut), cut)
        gt = mm_nt(mine_ref[1], wq_ref[part, :]) + mm_nt(got_ref[1], wqx_ref[part, :])
        at = mm(mine_ref[0], wo_ref[:, part]) + mm(got_ref[0], wox_ref[:, part])
        for i, r in enumerate((gt, at)):
            for j in range(XS):
                out_refs[j][i, :, part] = r[j * rows : (j + 1) * rows].astype(BF)
        return 0

    lax.fori_loop(0, steps, step, 0)


def outs(mine, got, w_query, wx_query, w_out, wx_out):
    _, length, width = mine.shape
    full = w_query.shape[0]
    cut = full // 8
    return pl.pallas_call(
        functools.partial(outs_kernel, cut=cut),
        in_specs=[ANY] * 6,
        out_specs=[VMEM] * XS,
        scratch_shapes=[
            pltpu.VMEM(mine.shape, BF),
            pltpu.VMEM(mine.shape, BF),
            pltpu.VMEM(w_query.shape, BF),
            pltpu.VMEM(w_query.shape, BF),
            pltpu.VMEM(w_out.shape, BF),
            pltpu.VMEM(w_out.shape, BF),
            pltpu.SemaphoreType.DMA((4 * (full // cut) + 2,)),
        ],
        out_shape=[jax.ShapeDtypeStruct((2, length // XS, full), BF)] * XS,
        compiler_params=params(B_OUTS),
        cost_estimate=cost(int(OUTS * 8 * length * width * full), int(OUTS * (16 << 20))),
        name="outs",
    )(mine, got, w_query, wx_query, w_out, wx_out)


def pick_kernel(index_ref, table_ref, *out_refs):
    at = 0
    for out in out_refs:
        for i in range(out.shape[0]):
            out[i] = table_ref[index_ref[at]]
            at += 1


def pick(index, table, counts, name):
    rest = table.shape[1:]
    return pl.pallas_call(
        pick_kernel,
        in_specs=[SMEM, VMEM],
        out_specs=[VMEM] * len(counts),
        out_shape=[jax.ShapeDtypeStruct((n, *rest), table.dtype) for n in counts],
        compiler_params=params(16),
        cost_estimate=cost(0, 1 << 20),
        name=name,
    )(index, table)


def outgoing_kernel(slot_ref, at_ref, table_any, out_ref, part, sem):
    cols = out_ref.shape[2]
    at = pl.ds(pl.multiple_of(at_ref[0] * cols, cols), cols)
    copy = pltpu.make_async_copy(table_any.at[:, :, at], part, sem)
    copy.start()
    copy.wait()
    for i in range(out_ref.shape[0]):
        out_ref[i] = part[slot_ref[i]]


def choose_outgoing(slot, at, table, cols):
    count, depth, _ = table.shape
    return pl.pallas_call(
        outgoing_kernel,
        in_specs=[SMEM, SMEM, ANY],
        out_specs=VMEM,
        scratch_shapes=[pltpu.VMEM((count, depth, cols), BF), pltpu.SemaphoreType.DMA(())],
        out_shape=jax.ShapeDtypeStruct((slot.shape[0], depth, cols), BF),
        compiler_params=params(BIG),
        cost_estimate=cost(0, 1 << 20),
        name="outgoing",
    )(slot, at, table)


def place_kernel(owner_ref, *refs):
    parts, out_ref = refs[:-1], refs[-1]
    for e in range(parts[0].shape[0]):
        total = parts[0][e].astype(F32)
        for part in parts[1:]:
            total = total + part[e].astype(F32)
        out_ref[owner_ref[e]] = total.astype(BF)


def place_sums(owner, parts, count):
    return pl.pallas_call(
        place_kernel,
        in_specs=[SMEM] + [VMEM] * len(parts),
        out_specs=VMEM,
        out_shape=jax.ShapeDtypeStruct((count, *parts[0].shape[1:]), BF),
        compiler_params=params(16),
        cost_estimate=cost(0, 4 << 20),
        name="place",
    )(owner, *parts)


def collect_kernel(slot_ref, held_ref, in_ref, out_ref):
    out_ref[...] = jnp.zeros(out_ref.shape, F32)
    for i in range(in_ref.shape[0]):

        @pl.when(held_ref[i] > 0)
        def _():
            out_ref[slot_ref[i]] += in_ref[i].astype(F32)


def collect(slot, held, returned, count):
    rest = returned.shape[1:]
    return pl.pallas_call(
        collect_kernel,
        in_specs=[SMEM, SMEM, VMEM],
        out_specs=VMEM,
        out_shape=jax.ShapeDtypeStruct((count, *rest), F32),
        compiler_params=params(16),
        cost_estimate=cost(0, 2 << 20),
        name="collect",
    )(slot, held, returned)


def final_kernel(*refs):
    parts, (out0, out1, total, sems) = refs[:XS], refs[XS:]
    cut = total.shape[2] // 4
    copies = []
    for k in range(4):
        part = pl.ds(k * cut, cut)
        sums = parts[0][:, :, part].astype(F32)
        for r in parts[1:]:
            sums = sums + r[:, :, part].astype(F32)
        total[:, :, part] = sums.astype(BF)
        for i, out in enumerate((out0, out1)):
            src = total.at[i, :, part]
            copies.append(pltpu.make_async_copy(src, out.at[:, part], sems.at[2 * k + i]))
            copies[-1].start()
    for copy in copies:
        copy.wait()


def final_sums(parts):
    _, rows, full = parts[0].shape
    out = jax.ShapeDtypeStruct((rows, full), BF)
    return pl.pallas_call(
        final_kernel,
        in_specs=[VMEM] * XS,
        out_specs=[ANY] * 2,
        scratch_shapes=[pltpu.VMEM(parts[0].shape, BF), pltpu.SemaphoreType.DMA((8,))],
        out_shape=[out, out],
        compiler_params=params(16),
        cost_estimate=cost(LAST << 20, 4 << 20),
        name="final",
    )(*parts)


def chip_sums(keep, got):
    return [(keep[i].astype(F32) + got[i].astype(F32)).astype(BF) for i in range(XS)]


def x_parts(sums):
    return sums[:1] + [lax.ppermute(sums[i], "mp", x_perm(i)) for i in range(1, XS)]


def body(
    tokens, encoded, neighbour_owner, neighbour_slot, w_query, w_key, w_value, w_out, grad_out
):
    dp_count = lax.axis_size("dp")
    dp_at = lax.axis_index("dp")
    mp_at = lax.axis_index("mp")
    x, c = mp_at // CORES, mp_at % CORES
    neigh = neighbour_owner.shape[1] * NBR
    share = encoded.shape[2] // (XS * CORES)
    indices = by_distance(x, c)

    owners_all = neighbour_owner.reshape(dp_count, neigh)
    slots_all = neighbour_slot.reshape(dp_count, neigh)
    held_here = owners_all == dp_at
    held = jnp.any(held_here, axis=1).astype(jnp.int32)
    held_slot = jnp.sum(jnp.where(held_here, slots_all, 0), axis=1).astype(jnp.int32)
    my_owners = lax.dynamic_index_in_dim(owners_all, dp_at, 0, keepdims=False)
    t_own = x_pieces(tokens)
    g_own = x_pieces(grad_out)
    outgoing = choose_outgoing(held_slot, mp_at[None].astype(jnp.int32), encoded, share)
    arrived = lax.all_to_all(outgoing, "dp", split_axis=0, concat_axis=0, tiled=True)
    wx_query, wx_out = swap(w_query), swap(w_out)
    q_own, q_send = project(
        t_own, w_query, wx_query, False, "query", FIRST
    )
    q_got = swap(q_send)
    w_key, w_value = arrange(indices, after(w_key, q_own), w_value)
    (near,) = pick(my_owners, after(arrived, (q_own, q_got, g_own, w_key)), [neigh], "nearby")
    gh_own, gh_send = project(after(g_own, near), w_out, wx_out, True, "gheads", 0)
    near = x_pieces(near)
    gh_got = swap(gh_send)
    query, grad_heads = assemble(indices, (q_own, q_got), (gh_own, gh_got))
    own = [after(piece, grad_heads) for piece in near]
    pieces = own + [swap(piece) for piece in own]
    mine, theirs, keep, send = attend(indices, pieces, query, grad_heads, w_key, w_value)
    sums = chip_sums(keep, swap(send))
    parts = [x_parts(sums)]
    sums2 = list(
        outs(after(mine, sums), swap(theirs), w_query, wx_query, w_out, wx_out)
    )
    parts2 = x_parts(after(sums2, parts))
    parts = after(parts, sums2)
    returned = lax.all_to_all(
        place_sums(my_owners, parts[0], dp_count), "dp", split_axis=0, concat_axis=0, tiled=True
    )
    grad_tokens, attended = final_sums(parts2)
    grad_encoded = collect(held_slot, held, after(returned, attended), encoded.shape[0])
    return (attended, grad_tokens, grad_encoded)


def solution(mesh):
    placed = (
        P(("dp", "mp"), None),
        P("dp", None, None),
        P(),
        P(),
        P(None, "mp"),
        P(None, "mp"),
        P(None, "mp"),
        P("mp", None),
        P(("dp", "mp"), None),
    )
    return jax.shard_map(
        body,
        mesh=mesh,
        in_specs=placed,
        out_specs=(P(("dp", "mp"), None), P(("dp", "mp"), None), P("dp", None, "mp")),
        check_vma=False,
    )
```

```python
import functools
import math

import jax
import jax.numpy as jnp
from jax import lax
from jax.experimental import pallas as pl
from jax.experimental.pallas import tpu as pltpu
from jax.sharding import PartitionSpec as P

HD = 128
GROUP = 64
NBR = 2
XS = 4
CORES = 2
BF = jnp.bfloat16
F32 = jnp.float32
BIG = 56
B_PROJ = 56
B_ATT = 30
B_OUTS = 30
FIRST = 16
OUTS = 0.3
LAST = 65536
ATT = 1
NT = (((1,), (1,)), ((), ()))
TN = (((0,), (0,)), ((), ()))


def mm(a, b):
    return jnp.dot(a, b, preferred_element_type=F32)


def mm_nt(a, b):
    return lax.dot_general(a, b, NT, preferred_element_type=F32)


def mm_tn(a, b):
    return lax.dot_general(a, b, TN, preferred_element_type=F32)


def x_perm(step):
    return [(2 * x + c, 2 * ((x + step) % XS) + c) for x in range(XS) for c in range(CORES)]


CORE_SWAP = [(2 * x + c, 2 * x + 1 - c) for x in range(XS) for c in range(CORES)]


def x_pieces(block):
    return [block] + [lax.ppermute(block, "mp", x_perm(-i)) for i in range(1, XS)]


def swap(block):
    return lax.ppermute(block, "mp", CORE_SWAP)


def after(values, earlier):
    return lax.optimization_barrier((values, earlier))[0]


def by_distance(x, c):
    own = [2 * ((x + i) % XS) + c for i in range(XS)]
    other = [2 * ((x + i) % XS) + 1 - c for i in range(XS)]
    return jnp.stack(own + other).astype(jnp.int32)


ANY = pl.BlockSpec(memory_space=pl.ANY)
SMEM = pl.BlockSpec(memory_space=pltpu.SMEM)
VMEM = pl.BlockSpec(memory_space=pltpu.VMEM)


def params(mib):
    return pltpu.CompilerParams(vmem_limit_bytes=mib << 20)


def cost(flops, bytes_accessed):
    return pl.CostEstimate(flops=flops, bytes_accessed=bytes_accessed, transcendentals=0)


def project_kernel(*refs, cut, transposed):
    pieces = refs[:4]
    w_any, wx_any, out_ref, outx_ref, a_ref, w_ref, wx_ref, acc, accx, sems = refs[4:]
    rows = pieces[0].shape[0]
    steps = a_ref.shape[1] // cut
    copies = []
    for j, piece in enumerate(pieces):
        at = pl.ds(j * rows, rows)
        copies.append(pltpu.make_async_copy(piece, a_ref.at[at, :], sems.at[j]))
        copies[-1].start()

    def weights(k):
        part = pl.ds(pl.multiple_of(k * cut, cut), cut)
        at = (slice(None), part) if transposed else (part, slice(None))
        return [
            pltpu.make_async_copy(w_any.at[at], w_ref.at[at], sems.at[4 + 2 * k]),
            pltpu.make_async_copy(wx_any.at[at], wx_ref.at[at], sems.at[5 + 2 * k]),
        ]

    for k in range(steps):
        for copy in weights(k):
            copy.start()
    acc[...] = jnp.zeros(acc.shape, F32)
    accx[...] = jnp.zeros(accx.shape, F32)
    for copy in copies:
        copy.wait()

    def step(k, _):
        part = pl.ds(pl.multiple_of(k * cut, cut), cut)
        a = a_ref[:, part]
        for copy, w, total in zip(weights(k), (w_ref, wx_ref), (acc, accx)):
            copy.wait()
            total[...] += mm_nt(a, w[:, part]) if transposed else mm(a, w[part, :])
        return 0

    lax.fori_loop(0, steps, step, 0)
    out_ref[...] = acc[...].astype(BF)
    outx_ref[...] = accx[...].astype(BF)


def project(pieces, w, wx, transposed, name, weight=1):
    rows, depth = pieces[0].shape
    width = w.shape[0] if transposed else w.shape[1]
    length = rows * len(pieces)
    cut = depth // 8
    out = jax.ShapeDtypeStruct((length, width), BF)
    return pl.pallas_call(
        functools.partial(project_kernel, cut=cut, transposed=transposed),
        in_specs=[ANY] * 6,
        out_specs=[VMEM] * 2,
        scratch_shapes=[
            pltpu.VMEM((length, depth), BF),
            pltpu.VMEM(w.shape, BF),
            pltpu.VMEM(w.shape, BF),
            pltpu.VMEM((length, width), F32),
            pltpu.VMEM((length, width), F32),
            pltpu.SemaphoreType.DMA((4 + 2 * (depth // cut),)),
        ],
        out_shape=[out, out],
        compiler_params=params(B_PROJ),
        cost_estimate=cost(int(4 * length * depth * width * weight), 1 << 20),
        name=name,
    )(*pieces, w, wx)


def arrange_kernel(index_ref, wk_any, wv_any, wk_out, wv_out, sems):
    rows = wk_any.shape[0] // 8
    copies = []
    for j in range(8):
        at = pl.ds(pl.multiple_of(index_ref[j] * rows, rows), rows)
        put = pl.ds(j * rows, rows)
        for i, (w, o) in enumerate(((wk_any, wk_out), (wv_any, wv_out))):
            copies.append(pltpu.make_async_copy(w.at[at, :], o.at[put, :], sems.at[2 * j + i]))
            copies[-1].start()
    for copy in copies:
        copy.wait()


def arrange(indices, w_key, w_value):
    out = jax.ShapeDtypeStruct(w_key.shape, BF)
    return pl.pallas_call(
        arrange_kernel,
        in_specs=[SMEM, ANY, ANY],
        out_specs=[ANY] * 2,
        scratch_shapes=[pltpu.SemaphoreType.DMA((16,))],
        out_shape=[out, out],
        compiler_params=params(8),
        cost_estimate=cost(0, 1 << 20),
        name="arrange",
    )(indices, w_key, w_value)


def assemble_kernel(index_ref, *refs):
    parts, outs_ref = refs[:4], refs[4:]
    rows = outs_ref[0].shape[0] // 8
    for i in range(2):
        for j in range(8):
            at = pl.ds(pl.multiple_of(index_ref[j] * rows, 16), rows)
            part = slice(j % XS * rows, (j % XS + 1) * rows)
            outs_ref[i][at, :] = parts[2 * i + j // XS][part, :]


def assemble(indices, q, gh):
    out = jax.ShapeDtypeStruct((2 * q[0].shape[0], q[0].shape[1]), BF)
    return pl.pallas_call(
        assemble_kernel,
        in_specs=[SMEM] + [VMEM] * 4,
        out_specs=[VMEM] * 2,
        out_shape=[out, out],
        compiler_params=params(8),
        cost_estimate=cost(0, 1 << 20),
        name="assemble",
    )(indices, *q, *gh)


def attend_kernel(index_ref, *refs):
    pieces = refs[:8]
    q_ref, gh_ref, wk_ref, wv_ref, mine_ref, theirs_ref, keep_ref, send_ref, small = refs[8:]
    neigh, depth, cols = pieces[0].shape
    groups = neigh // NBR
    keys = NBR * depth
    heads = q_ref.shape[1] // HD
    scale = 1.0 / math.sqrt(HD)
    part = [slice(h * HD, (h + 1) * HD) for h in range(heads)]

    def group(g, _):
        own = pl.ds(pl.multiple_of(g * GROUP, GROUP), GROUP)
        two = pl.ds(g * NBR, NBR)

        near_rows = jnp.concatenate([p[two].reshape(keys, cols) for p in pieces], axis=1)
        k = mm(near_rows, wk_ref[...]).astype(BF)
        v = mm(near_rows, wv_ref[...]).astype(BF)
        q = q_ref[own, :]
        gh = gh_ref[own, :]
        s = jnp.concatenate([mm_nt(q[:, p], k[:, p]) for p in part], axis=0) * scale
        gp = jnp.concatenate([mm_nt(gh[:, p], v[:, p]) for p in part], axis=0)
        e = jnp.exp(s - jnp.max(s, axis=-1, keepdims=True))
        probs = e * (1.0 / jnp.sum(e, axis=-1, keepdims=True))
        pb = probs.astype(BF)
        centre = jnp.sum(probs * gp, axis=-1, keepdims=True)
        gs = (probs * (gp - centre) * scale).astype(BF)
        gk = []
        gv = []
        for h, p in enumerate(part):
            r = slice(h * GROUP, (h + 1) * GROUP)
            small[0, own, p] = mm(pb[r], v[:, p]).astype(BF)
            small[1, own, p] = mm(gs[r], k[:, p]).astype(BF)
            gk.append(mm_tn(gs[r], q[:, p]).astype(BF))
            gv.append(mm_tn(pb[r], gh[:, p]).astype(BF))
        gk = jnp.concatenate(gk, axis=1)
        gv = jnp.concatenate(gv, axis=1)
        for j in range(0, 8, 2):
            put = slice(j * cols, (j + 2) * cols)
            grad = (mm_nt(gk, wk_ref[put, :]) + mm_nt(gv, wv_ref[put, :])).astype(BF)
            for i in range(2):
                ref = (keep_ref, send_ref)[(j + i) // XS]
                ref[(j + i) % XS, two] = grad[:, i * cols : (i + 1) * cols].reshape(NBR, depth, cols)
        return 0

    lax.fori_loop(0, groups, group, 0, unroll=2)
    rows = small.shape[1] // 8
    for j in range(8):
        at = pl.ds(pl.multiple_of(index_ref[j] * rows, 16), rows)
        put = slice(j % XS * rows, (j % XS + 1) * rows)
        (mine_ref, theirs_ref)[j // XS][:, put, :] = small[:, at, :]


def attend(indices, pieces, q, gh, w_key, w_value):
    neigh, depth, cols = pieces[0].shape
    length, width = q.shape
    share = jax.ShapeDtypeStruct((XS, neigh, depth, cols), BF)
    half = jax.ShapeDtypeStruct((2, length // 2, width), BF)
    return pl.pallas_call(
        attend_kernel,
        in_specs=[SMEM] + [VMEM] * 12,
        out_specs=[VMEM] * 4,
        scratch_shapes=[pltpu.VMEM((2, length, width), BF)],
        out_shape=[half, half, share, share],
        compiler_params=params(B_ATT),
        cost_estimate=cost(int(ATT * 8 * neigh * depth * 8 * cols * width), 1 << 20),
        name="attend",
    )(indices, *pieces, q, gh, w_key, w_value)


def outs_kernel(mine_any, got_any, wq_any, wqx_any, wo_any, wox_any, *refs, cut):
    out_refs, (mine_ref, got_ref, wq_ref, wqx_ref, wo_ref, wox_ref, sems) = refs[:XS], refs[XS:]
    rows = mine_ref.shape[1] // XS
    steps = wq_ref.shape[0] // cut
    first = [
        pltpu.make_async_copy(mine_any, mine_ref, sems.at[4 * steps]),
        pltpu.make_async_copy(got_any, got_ref, sems.at[4 * steps + 1]),
    ]

    def weights(k):
        part = pl.ds(pl.multiple_of(k * cut, cut), cut)
        moves = [(w.at[part, :], r.at[part, :]) for w, r in ((wq_any, wq_ref), (wqx_any, wqx_ref))]
        moves += [(w.at[:, part], r.at[:, part]) for w, r in ((wo_any, wo_ref), (wox_any, wox_ref))]
        return [pltpu.make_async_copy(s, d, sems.at[4 * k + i]) for i, (s, d) in enumerate(moves)]

    for copy in first:
        copy.start()
    for k in range(steps):
        for copy in weights(k):
            copy.start()
    for copy in first:
        copy.wait()

    def step(k, _):
        for copy in weights(k):
            copy.wait()
        part = pl.ds(pl.multiple_of(k * cut, cut), cut)
        gt = mm_nt(mine_ref[1], wq_ref[part, :]) + mm_nt(got_ref[1], wqx_ref[part, :])
        at = mm(mine_ref[0], wo_ref[:, part]) + mm(got_ref[0], wox_ref[:, part])
        for i, r in enumerate((gt, at)):
            for j in range(XS):
                out_refs[j][i, :, part] = r[j * rows : (j + 1) * rows].astype(BF)
        return 0

    lax.fori_loop(0, steps, step, 0)


def outs(mine, got, w_query, wx_query, w_out, wx_out):
    _, length, width = mine.shape
    full = w_query.shape[0]
    cut = full // 8
    return pl.pallas_call(
        functools.partial(outs_kernel, cut=cut),
        in_specs=[ANY] * 6,
        out_specs=[VMEM] * XS,
        scratch_shapes=[
            pltpu.VMEM(mine.shape, BF),
            pltpu.VMEM(mine.shape, BF),
            pltpu.VMEM(w_query.shape, BF),
            pltpu.VMEM(w_query.shape, BF),
            pltpu.VMEM(w_out.shape, BF),
            pltpu.VMEM(w_out.shape, BF),
            pltpu.SemaphoreType.DMA((4 * (full // cut) + 2,)),
        ],
        out_shape=[jax.ShapeDtypeStruct((2, length // XS, full), BF)] * XS,
        compiler_params=params(B_OUTS),
        cost_estimate=cost(int(OUTS * 8 * length * width * full), int(OUTS * (16 << 20))),
        name="outs",
    )(mine, got, w_query, wx_query, w_out, wx_out)


def pick_kernel(index_ref, table_ref, *out_refs):
    at = 0
    for out in out_refs:
        for i in range(out.shape[0]):
            out[i] = table_ref[index_ref[at]]
            at += 1


def pick(index, table, counts, name):
    rest = table.shape[1:]
    return pl.pallas_call(
        pick_kernel,
        in_specs=[SMEM, VMEM],
        out_specs=[VMEM] * len(counts),
        out_shape=[jax.ShapeDtypeStruct((n, *rest), table.dtype) for n in counts],
        compiler_params=params(16),
        cost_estimate=cost(0, 1 << 20),
        name=name,
    )(index, table)


def outgoing_kernel(slot_ref, at_ref, table_any, out_ref, part, sem):
    cols = out_ref.shape[2]
    at = pl.ds(pl.multiple_of(at_ref[0] * cols, cols), cols)
    copy = pltpu.make_async_copy(table_any.at[:, :, at], part, sem)
    copy.start()
    copy.wait()
    for i in range(out_ref.shape[0]):
        out_ref[i] = part[slot_ref[i]]


def choose_outgoing(slot, at, table, cols):
    count, depth, _ = table.shape
    return pl.pallas_call(
        outgoing_kernel,
        in_specs=[SMEM, SMEM, ANY],
        out_specs=VMEM,
        scratch_shapes=[pltpu.VMEM((count, depth, cols), BF), pltpu.SemaphoreType.DMA(())],
        out_shape=jax.ShapeDtypeStruct((slot.shape[0], depth, cols), BF),
        compiler_params=params(BIG),
        cost_estimate=cost(0, 1 << 20),
        name="outgoing",
    )(slot, at, table)


def place_kernel(owner_ref, *refs):
    parts, out_ref = refs[:-1], refs[-1]
    for e in range(parts[0].shape[0]):
        total = parts[0][e].astype(F32)
        for part in parts[1:]:
            total = total + part[e].astype(F32)
        out_ref[owner_ref[e]] = total.astype(BF)


def place_sums(owner, parts, count):
    return pl.pallas_call(
        place_kernel,
        in_specs=[SMEM] + [VMEM] * len(parts),
        out_specs=VMEM,
        out_shape=jax.ShapeDtypeStruct((count, *parts[0].shape[1:]), BF),
        compiler_params=params(16),
        cost_estimate=cost(0, 4 << 20),
        name="place",
    )(owner, *parts)


def collect_kernel(slot_ref, held_ref, in_ref, out_ref):
    out_ref[...] = jnp.zeros(out_ref.shape, F32)
    for i in range(in_ref.shape[0]):

        @pl.when(held_ref[i] > 0)
        def _():
            out_ref[slot_ref[i]] += in_ref[i].astype(F32)


def collect(slot, held, returned, count):
    rest = returned.shape[1:]
    return pl.pallas_call(
        collect_kernel,
        in_specs=[SMEM, SMEM, VMEM],
        out_specs=VMEM,
        out_shape=jax.ShapeDtypeStruct((count, *rest), F32),
        compiler_params=params(16),
        cost_estimate=cost(0, 2 << 20),
        name="collect",
    )(slot, held, returned)


def final_kernel(*refs):
    parts, (out0, out1, total, sems) = refs[:XS], refs[XS:]
    cut = total.shape[2] // 4
    copies = []
    for k in range(4):
        part = pl.ds(k * cut, cut)
        sums = parts[0][:, :, part].astype(F32)
        for r in parts[1:]:
            sums = sums + r[:, :, part].astype(F32)
        total[:, :, part] = sums.astype(BF)
        for i, out in enumerate((out0, out1)):
            src = total.at[i, :, part]
            copies.append(pltpu.make_async_copy(src, out.at[:, part], sems.at[2 * k + i]))
            copies[-1].start()
    for copy in copies:
        copy.wait()


def final_sums(parts):
    _, rows, full = parts[0].shape
    out = jax.ShapeDtypeStruct((rows, full), BF)
    return pl.pallas_call(
        final_kernel,
        in_specs=[VMEM] * XS,
        out_specs=[ANY] * 2,
        scratch_shapes=[pltpu.VMEM(parts[0].shape, BF), pltpu.SemaphoreType.DMA((8,))],
        out_shape=[out, out],
        compiler_params=params(16),
        cost_estimate=cost(LAST << 20, 4 << 20),
        name="final",
    )(*parts)


def chip_sums(keep, got):
    return [(keep[i].astype(F32) + got[i].astype(F32)).astype(BF) for i in range(XS)]


def x_parts(sums):
    return sums[:1] + [lax.ppermute(sums[i], "mp", x_perm(i)) for i in range(1, XS)]


def body(
    tokens, encoded, neighbour_owner, neighbour_slot, w_query, w_key, w_value, w_out, grad_out
):
    dp_count = lax.axis_size("dp")
    dp_at = lax.axis_index("dp")
    mp_at = lax.axis_index("mp")
    x, c = mp_at // CORES, mp_at % CORES
    neigh = neighbour_owner.shape[1] * NBR
    share = encoded.shape[2] // (XS * CORES)
    indices = by_distance(x, c)

    owners_all = neighbour_owner.reshape(dp_count, neigh)
    slots_all = neighbour_slot.reshape(dp_count, neigh)
    held_here = owners_all == dp_at
    held = jnp.any(held_here, axis=1).astype(jnp.int32)
    held_slot = jnp.sum(jnp.where(held_here, slots_all, 0), axis=1).astype(jnp.int32)
    my_owners = lax.dynamic_index_in_dim(owners_all, dp_at, 0, keepdims=False)
    t_own = x_pieces(tokens)
    g_own = x_pieces(grad_out)
    outgoing = choose_outgoing(held_slot, mp_at[None].astype(jnp.int32), encoded, share)
    arrived = lax.all_to_all(outgoing, "dp", split_axis=0, concat_axis=0, tiled=True)
    wx_query, wx_out = swap(w_query), swap(w_out)
    q_own, q_send = project(
        t_own, w_query, wx_query, False, "query", FIRST
    )
    q_got = swap(q_send)
    w_key, w_value = arrange(indices, after(w_key, q_own), w_value)
    (near,) = pick(my_owners, after(arrived, (q_own, q_got, g_own, w_key)), [neigh], "nearby")
    gh_own, gh_send = project(after(g_own, near), w_out, wx_out, True, "gheads", 0)
    near = x_pieces(near)
    gh_got = swap(gh_send)
    query, grad_heads = assemble(indices, (q_own, q_got), (gh_own, gh_got))
    own = [after(piece, grad_heads) for piece in near]
    pieces = own + [swap(piece) for piece in own]
    mine, theirs, keep, send = attend(indices, pieces, query, grad_heads, w_key, w_value)
    sums = chip_sums(keep, swap(send))
    parts = [x_parts(sums)]
    sums2 = list(
        outs(after(mine, sums), swap(theirs), w_query, wx_query, w_out, wx_out)
    )
    parts2 = x_parts(after(sums2, parts))
    parts = after(parts, sums2)
    returned = lax.all_to_all(
        place_sums(my_owners, parts[0], dp_count), "dp", split_axis=0, concat_axis=0, tiled=True
    )
    grad_tokens, attended = final_sums(parts2)
    grad_encoded = collect(held_slot, held, after(returned, attended), encoded.shape[0])
    return (attended, grad_tokens, grad_encoded)


def solution(mesh):
    placed = (
        P(("dp", "mp"), None),
        P("dp", None, None),
        P(),
        P(),
        P(None, "mp"),
        P(None, "mp"),
        P(None, "mp"),
        P("mp", None),
        P(("dp", "mp"), None),
    )
    return jax.shard_map(
        body,
        mesh=mesh,
        in_specs=placed,
        out_specs=(P(("dp", "mp"), None), P(("dp", "mp"), None), P("dp", None, "mp")),
        check_vma=False,
    )
```

```python
import functools
import math

import jax
import jax.numpy as jnp
from jax import lax
from jax.experimental import pallas as pl
from jax.experimental.pallas import tpu as pltpu
from jax.sharding import PartitionSpec as P

HD = 128
GROUP = 64
NBR = 2
XS = 4
CORES = 2
BF = jnp.bfloat16
F32 = jnp.float32
BIG = 56
B_PROJ = 56
B_ATT = 30
B_OUTS = 30
FIRST = 16
OUTS = 0.3
LAST = 65536
ATT = 1
NT = (((1,), (1,)), ((), ()))
TN = (((0,), (0,)), ((), ()))


def mm(a, b):
    return jnp.dot(a, b, preferred_element_type=F32)


def mm_nt(a, b):
    return lax.dot_general(a, b, NT, preferred_element_type=F32)


def mm_tn(a, b):
    return lax.dot_general(a, b, TN, preferred_element_type=F32)


def x_perm(step):
    return [(2 * x + c, 2 * ((x + step) % XS) + c) for x in range(XS) for c in range(CORES)]


CORE_SWAP = [(2 * x + c, 2 * x + 1 - c) for x in range(XS) for c in range(CORES)]


def x_pieces(block):
    return [block] + [lax.ppermute(block, "mp", x_perm(-i)) for i in range(1, XS)]


def swap(block):
    return lax.ppermute(block, "mp", CORE_SWAP)


def after(values, earlier):
    return lax.optimization_barrier((values, earlier))[0]


def by_distance(x, c):
    own = [2 * ((x + i) % XS) + c for i in range(XS)]
    other = [2 * ((x + i) % XS) + 1 - c for i in range(XS)]
    return jnp.stack(own + other).astype(jnp.int32)


ANY = pl.BlockSpec(memory_space=pl.ANY)
SMEM = pl.BlockSpec(memory_space=pltpu.SMEM)
VMEM = pl.BlockSpec(memory_space=pltpu.VMEM)


def params(mib):
    return pltpu.CompilerParams(vmem_limit_bytes=mib << 20)


def cost(flops, bytes_accessed):
    return pl.CostEstimate(flops=flops, bytes_accessed=bytes_accessed, transcendentals=0)


def project_kernel(*refs, cut, transposed):
    pieces = refs[:4]
    w_any, wx_any, out_ref, outx_ref, a_ref, w_ref, wx_ref, acc, accx, sems = refs[4:]
    rows = pieces[0].shape[0]
    steps = a_ref.shape[1] // cut
    copies = []
    for j, piece in enumerate(pieces):
        at = pl.ds(j * rows, rows)
        copies.append(pltpu.make_async_copy(piece, a_ref.at[at, :], sems.at[j]))
        copies[-1].start()

    def weights(k):
        part = pl.ds(pl.multiple_of(k * cut, cut), cut)
        at = (slice(None), part) if transposed else (part, slice(None))
        return [
            pltpu.make_async_copy(w_any.at[at], w_ref.at[at], sems.at[4 + 2 * k]),
            pltpu.make_async_copy(wx_any.at[at], wx_ref.at[at], sems.at[5 + 2 * k]),
        ]

    for k in range(steps):
        for copy in weights(k):
            copy.start()
    acc[...] = jnp.zeros(acc.shape, F32)
    accx[...] = jnp.zeros(accx.shape, F32)
    for copy in copies:
        copy.wait()

    def step(k, _):
        part = pl.ds(pl.multiple_of(k * cut, cut), cut)
        a = a_ref[:, part]
        for copy, w, total in zip(weights(k), (w_ref, wx_ref), (acc, accx)):
            copy.wait()
            total[...] += mm_nt(a, w[:, part]) if transposed else mm(a, w[part, :])
        return 0

    lax.fori_loop(0, steps, step, 0)
    out_ref[...] = acc[...].astype(BF)
    outx_ref[...] = accx[...].astype(BF)


def project(pieces, w, wx, transposed, name, weight=1):
    rows, depth = pieces[0].shape
    width = w.shape[0] if transposed else w.shape[1]
    length = rows * len(pieces)
    cut = depth // 8
    out = jax.ShapeDtypeStruct((length, width), BF)
    return pl.pallas_call(
        functools.partial(project_kernel, cut=cut, transposed=transposed),
        in_specs=[VMEM] * 2 + [ANY] * 4,
        out_specs=[VMEM] * 2,
        scratch_shapes=[
            pltpu.VMEM((length, depth), BF),
            pltpu.VMEM(w.shape, BF),
            pltpu.VMEM(w.shape, BF),
            pltpu.VMEM((length, width), F32),
            pltpu.VMEM((length, width), F32),
            pltpu.SemaphoreType.DMA((4 + 2 * (depth // cut),)),
        ],
        out_shape=[out, out],
        compiler_params=params(B_PROJ),
        cost_estimate=cost(int(4 * length * depth * width * weight), 1 << 20),
        name=name,
    )(*pieces, w, wx)


def arrange_kernel(index_ref, wk_any, wv_any, wk_out, wv_out, sems):
    rows = wk_any.shape[0] // 8
    copies = []
    for j in range(8):
        at = pl.ds(pl.multiple_of(index_ref[j] * rows, rows), rows)
        put = pl.ds(j * rows, rows)
        for i, (w, o) in enumerate(((wk_any, wk_out), (wv_any, wv_out))):
            copies.append(pltpu.make_async_copy(w.at[at, :], o.at[put, :], sems.at[2 * j + i]))
            copies[-1].start()
    for copy in copies:
        copy.wait()


def arrange(indices, w_key, w_value):
    out = jax.ShapeDtypeStruct(w_key.shape, BF)
    return pl.pallas_call(
        arrange_kernel,
        in_specs=[SMEM, ANY, ANY],
        out_specs=[ANY] * 2,
        scratch_shapes=[pltpu.SemaphoreType.DMA((16,))],
        out_shape=[out, out],
        compiler_params=params(8),
        cost_estimate=cost(0, 1 << 20),
        name="arrange",
    )(indices, w_key, w_value)


def assemble_kernel(index_ref, *refs):
    parts, outs_ref = refs[:4], refs[4:]
    rows = outs_ref[0].shape[0] // 8
    for i in range(2):
        for j in range(8):
            at = pl.ds(pl.multiple_of(index_ref[j] * rows, 16), rows)
            part = slice(j % XS * rows, (j % XS + 1) * rows)
            outs_ref[i][at, :] = parts[2 * i + j // XS][part, :]


def assemble(indices, q, gh):
    out = jax.ShapeDtypeStruct((2 * q[0].shape[0], q[0].shape[1]), BF)
    return pl.pallas_call(
        assemble_kernel,
        in_specs=[SMEM] + [VMEM] * 4,
        out_specs=[VMEM] * 2,
        out_shape=[out, out],
        compiler_params=params(8),
        cost_estimate=cost(0, 1 << 20),
        name="assemble",
    )(indices, *q, *gh)


def attend_kernel(index_ref, *refs):
    pieces = refs[:8]
    q_ref, gh_ref, wk_ref, wv_ref, mine_ref, theirs_ref, keep_ref, send_ref, small = refs[8:]
    neigh, depth, cols = pieces[0].shape
    groups = neigh // NBR
    keys = NBR * depth
    heads = q_ref.shape[1] // HD
    scale = 1.0 / math.sqrt(HD)
    part = [slice(h * HD, (h + 1) * HD) for h in range(heads)]

    def group(g, _):
        own = pl.ds(pl.multiple_of(g * GROUP, GROUP), GROUP)
        two = pl.ds(g * NBR, NBR)

        near_rows = jnp.concatenate([p[two].reshape(keys, cols) for p in pieces], axis=1)
        k = mm(near_rows, wk_ref[...]).astype(BF)
        v = mm(near_rows, wv_ref[...]).astype(BF)
        q = q_ref[own, :]
        gh = gh_ref[own, :]
        s = jnp.concatenate([mm_nt(q[:, p], k[:, p]) for p in part], axis=0) * scale
        gp = jnp.concatenate([mm_nt(gh[:, p], v[:, p]) for p in part], axis=0)
        e = jnp.exp(s - jnp.max(s, axis=-1, keepdims=True))
        probs = e * (1.0 / jnp.sum(e, axis=-1, keepdims=True))
        pb = probs.astype(BF)
        centre = jnp.sum(probs * gp, axis=-1, keepdims=True)
        gs = (probs * (gp - centre) * scale).astype(BF)
        gk = []
        gv = []
        for h, p in enumerate(part):
            r = slice(h * GROUP, (h + 1) * GROUP)
            small[0, own, p] = mm(pb[r], v[:, p]).astype(BF)
            small[1, own, p] = mm(gs[r], k[:, p]).astype(BF)
            gk.append(mm_tn(gs[r], q[:, p]).astype(BF))
            gv.append(mm_tn(pb[r], gh[:, p]).astype(BF))
        gk = jnp.concatenate(gk, axis=1)
        gv = jnp.concatenate(gv, axis=1)
        for j in range(0, 8, 2):
            put = slice(j * cols, (j + 2) * cols)
            grad = (mm_nt(gk, wk_ref[put, :]) + mm_nt(gv, wv_ref[put, :])).astype(BF)
            for i in range(2):
                ref = (keep_ref, send_ref)[(j + i) // XS]
                ref[(j + i) % XS, two] = grad[:, i * cols : (i + 1) * cols].reshape(NBR, depth, cols)
        return 0

    lax.fori_loop(0, groups, group, 0, unroll=2)
    rows = small.shape[1] // 8
    for j in range(8):
        at = pl.ds(pl.multiple_of(index_ref[j] * rows, 16), rows)
        put = slice(j % XS * rows, (j % XS + 1) * rows)
        (mine_ref, theirs_ref)[j // XS][:, put, :] = small[:, at, :]


def attend(indices, pieces, q, gh, w_key, w_value):
    neigh, depth, cols = pieces[0].shape
    length, width = q.shape
    share = jax.ShapeDtypeStruct((XS, neigh, depth, cols), BF)
    half = jax.ShapeDtypeStruct((2, length // 2, width), BF)
    return pl.pallas_call(
        attend_kernel,
        in_specs=[SMEM] + [VMEM] * 12,
        out_specs=[VMEM] * 4,
        scratch_shapes=[pltpu.VMEM((2, length, width), BF)],
        out_shape=[half, half, share, share],
        compiler_params=params(B_ATT),
        cost_estimate=cost(int(ATT * 8 * neigh * depth * 8 * cols * width), 1 << 20),
        name="attend",
    )(indices, *pieces, q, gh, w_key, w_value)


def outs_kernel(mine_ref, got_ref, wq_any, wqx_any, wo_any, wox_any, *refs, cut):
    out_refs, (wq_ref, wqx_ref, wo_ref, wox_ref, sems) = refs[:XS], refs[XS:]
    rows = mine_ref.shape[1] // XS
    steps = wq_ref.shape[0] // cut

    def weights(k):
        part = pl.ds(pl.multiple_of(k * cut, cut), cut)
        moves = [(w.at[part, :], r.at[part, :]) for w, r in ((wq_any, wq_ref), (wqx_any, wqx_ref))]
        moves += [(w.at[:, part], r.at[:, part]) for w, r in ((wo_any, wo_ref), (wox_any, wox_ref))]
        return [pltpu.make_async_copy(s, d, sems.at[4 * k + i]) for i, (s, d) in enumerate(moves)]

    for k in range(steps):
        for copy in weights(k):
            copy.start()

    def step(k, _):
        for copy in weights(k):
            copy.wait()
        part = pl.ds(pl.multiple_of(k * cut, cut), cut)
        gt = mm_nt(mine_ref[1], wq_ref[part, :]) + mm_nt(got_ref[1], wqx_ref[part, :])
        at = mm(mine_ref[0], wo_ref[:, part]) + mm(got_ref[0], wox_ref[:, part])
        for i, r in enumerate((gt, at)):
            for j in range(XS):
                out_refs[j][i, :, part] = r[j * rows : (j + 1) * rows].astype(BF)
        return 0

    lax.fori_loop(0, steps, step, 0)


def outs(mine, got, w_query, wx_query, w_out, wx_out):
    _, length, width = mine.shape
    full = w_query.shape[0]
    cut = full // 8
    return pl.pallas_call(
        functools.partial(outs_kernel, cut=cut),
        in_specs=[VMEM] * 2 + [ANY] * 4,
        out_specs=[VMEM] * XS,
        scratch_shapes=[
            pltpu.VMEM(w_query.shape, BF),
            pltpu.VMEM(w_query.shape, BF),
            pltpu.VMEM(w_out.shape, BF),
            pltpu.VMEM(w_out.shape, BF),
            pltpu.SemaphoreType.DMA((4 * (full // cut),)),
        ],
        out_shape=[jax.ShapeDtypeStruct((2, length // XS, full), BF)] * XS,
        compiler_params=params(B_OUTS),
        cost_estimate=cost(int(OUTS * 8 * length * width * full), int(OUTS * (16 << 20))),
        name="outs",
    )(mine, got, w_query, wx_query, w_out, wx_out)


def pick_kernel(index_ref, table_ref, *out_refs):
    at = 0
    for out in out_refs:
        for i in range(out.shape[0]):
            out[i] = table_ref[index_ref[at]]
            at += 1


def pick(index, table, counts, name):
    rest = table.shape[1:]
    return pl.pallas_call(
        pick_kernel,
        in_specs=[SMEM, VMEM],
        out_specs=[VMEM] * len(counts),
        out_shape=[jax.ShapeDtypeStruct((n, *rest), table.dtype) for n in counts],
        compiler_params=params(16),
        cost_estimate=cost(0, 1 << 20),
        name=name,
    )(index, table)


def outgoing_kernel(slot_ref, at_ref, table_any, out_ref, part, sem):
    cols = out_ref.shape[2]
    at = pl.ds(pl.multiple_of(at_ref[0] * cols, cols), cols)
    copy = pltpu.make_async_copy(table_any.at[:, :, at], part, sem)
    copy.start()
    copy.wait()
    for i in range(out_ref.shape[0]):
        out_ref[i] = part[slot_ref[i]]


def choose_outgoing(slot, at, table, cols):
    count, depth, _ = table.shape
    return pl.pallas_call(
        outgoing_kernel,
        in_specs=[SMEM, SMEM, ANY],
        out_specs=VMEM,
        scratch_shapes=[pltpu.VMEM((count, depth, cols), BF), pltpu.SemaphoreType.DMA(())],
        out_shape=jax.ShapeDtypeStruct((slot.shape[0], depth, cols), BF),
        compiler_params=params(16),
        cost_estimate=cost(0, 1 << 20),
        name="outgoing",
    )(slot, at, table)


def place_kernel(owner_ref, *refs):
    parts, out_ref = refs[:-1], refs[-1]
    for e in range(parts[0].shape[0]):
        total = parts[0][e].astype(F32)
        for part in parts[1:]:
            total = total + part[e].astype(F32)
        out_ref[owner_ref[e]] = total.astype(BF)


def place_sums(owner, parts, count):
    return pl.pallas_call(
        place_kernel,
        in_specs=[SMEM] + [VMEM] * len(parts),
        out_specs=VMEM,
        out_shape=jax.ShapeDtypeStruct((count, *parts[0].shape[1:]), BF),
        compiler_params=params(16),
        cost_estimate=cost(0, 4 << 20),
        name="place",
    )(owner, *parts)


def collect_kernel(slot_ref, held_ref, in_ref, out_ref):
    out_ref[...] = jnp.zeros(out_ref.shape, F32)
    for i in range(in_ref.shape[0]):

        @pl.when(held_ref[i] > 0)
        def _():
            out_ref[slot_ref[i]] += in_ref[i].astype(F32)


def collect(slot, held, returned, count):
    rest = returned.shape[1:]
    return pl.pallas_call(
        collect_kernel,
        in_specs=[SMEM, SMEM, VMEM],
        out_specs=VMEM,
        out_shape=jax.ShapeDtypeStruct((count, *rest), F32),
        compiler_params=params(16),
        cost_estimate=cost(0, 2 << 20),
        name="collect",
    )(slot, held, returned)


def final_kernel(*refs):
    parts, (out0, out1, total, sems) = refs[:XS], refs[XS:]
    cut = total.shape[2] // 4
    copies = []
    for k in range(4):
        part = pl.ds(k * cut, cut)
        sums = parts[0][:, :, part].astype(F32)
        for r in parts[1:]:
            sums = sums + r[:, :, part].astype(F32)
        total[:, :, part] = sums.astype(BF)
        for i, out in enumerate((out0, out1)):
            src = total.at[i, :, part]
            copies.append(pltpu.make_async_copy(src, out.at[:, part], sems.at[2 * k + i]))
            copies[-1].start()
    for copy in copies:
        copy.wait()


def final_sums(parts):
    _, rows, full = parts[0].shape
    out = jax.ShapeDtypeStruct((rows, full), BF)
    return pl.pallas_call(
        final_kernel,
        in_specs=[VMEM] * XS,
        out_specs=[ANY] * 2,
        scratch_shapes=[pltpu.VMEM(parts[0].shape, BF), pltpu.SemaphoreType.DMA((8,))],
        out_shape=[out, out],
        compiler_params=params(16),
        cost_estimate=cost(LAST << 20, 4 << 20),
        name="final",
    )(*parts)


def chip_sums(keep, got):
    return [(keep[i].astype(F32) + got[i].astype(F32)).astype(BF) for i in range(XS)]


def x_parts(sums):
    return sums[:1] + [lax.ppermute(sums[i], "mp", x_perm(i)) for i in range(1, XS)]


def body(
    tokens, encoded, neighbour_owner, neighbour_slot, w_query, w_key, w_value, w_out, grad_out
):
    dp_count = lax.axis_size("dp")
    dp_at = lax.axis_index("dp")
    mp_at = lax.axis_index("mp")
    x, c = mp_at // CORES, mp_at % CORES
    neigh = neighbour_owner.shape[1] * NBR
    share = encoded.shape[2] // (XS * CORES)
    indices = by_distance(x, c)

    owners_all = neighbour_owner.reshape(dp_count, neigh)
    slots_all = neighbour_slot.reshape(dp_count, neigh)
    held_here = owners_all == dp_at
    held = jnp.any(held_here, axis=1).astype(jnp.int32)
    held_slot = jnp.sum(jnp.where(held_here, slots_all, 0), axis=1).astype(jnp.int32)
    my_owners = lax.dynamic_index_in_dim(owners_all, dp_at, 0, keepdims=False)
    t_own = x_pieces(tokens)
    g_own = x_pieces(grad_out)
    outgoing = choose_outgoing(held_slot, mp_at[None].astype(jnp.int32), encoded, share)
    arrived = lax.all_to_all(outgoing, "dp", split_axis=0, concat_axis=0, tiled=True)
    wx_query, wx_out = swap(w_query), swap(w_out)
    q_own, q_send = project(
        t_own, w_query, wx_query, False, "query", FIRST
    )
    q_got = swap(q_send)
    w_key, w_value = arrange(indices, after(w_key, q_own), w_value)
    (near,) = pick(my_owners, after(arrived, (q_own, q_got, g_own, w_key)), [neigh], "nearby")
    gh_own, gh_send = project(after(g_own, near), w_out, wx_out, True, "gheads", 0)
    near = x_pieces(near)
    gh_got = swap(gh_send)
    query, grad_heads = assemble(indices, (q_own, q_got), (gh_own, gh_got))
    own = [after(piece, grad_heads) for piece in near]
    pieces = own + [swap(piece) for piece in own]
    mine, theirs, keep, send = attend(indices, pieces, query, grad_heads, w_key, w_value)
    sums = chip_sums(keep, swap(send))
    parts = [x_parts(sums)]
    sums2 = list(
        outs(after(mine, sums), swap(theirs), w_query, wx_query, w_out, wx_out)
    )
    parts2 = x_parts(after(sums2, parts))
    parts = after(parts, sums2)
    returned = lax.all_to_all(
        place_sums(my_owners, parts[0], dp_count), "dp", split_axis=0, concat_axis=0, tiled=True
    )
    grad_tokens, attended = final_sums(parts2)
    grad_encoded = collect(held_slot, held, after(returned, attended), encoded.shape[0])
    return (attended, grad_tokens, grad_encoded)


def solution(mesh):
    placed = (
        P(("dp", "mp"), None),
        P("dp", None, None),
        P(),
        P(),
        P(None, "mp"),
        P(None, "mp"),
        P(None, "mp"),
        P("mp", None),
        P(("dp", "mp"), None),
    )
    return jax.shard_map(
        body,
        mesh=mesh,
        in_specs=placed,
        out_specs=(P(("dp", "mp"), None), P(("dp", "mp"), None), P("dp", None, "mp")),
        check_vma=False,
    )
```
